256 devices in a mesh: row: 16 (over z_hi, y, core), col: 16 (over z_lo, x).
Axes of the slice: x: 4, y: 4, z: 8 (z_hi: 2, z_lo: 4; z = z_hi * 4 + z_lo), core: 2. Of those that a mesh axis runs over, the one named last changes fastest.
Arguments:
- single: bfloat16 [2048, 384], P('row', 'col'), may hold values from -6 to 6
- pair: bfloat16 [2048, 2048, 128], P('row', 'col'), may hold values from -6 to 6
- key_mask: int32 [2048], P('row'), may hold values 0 or 1
- chain: int32 [2048], P('row'), may hold values from 0 to 7, never falling along the last dimension, each value on 1 to 512 neighbouring positions
- single_gain: float32 [384], replicated, may hold values from 0.25 to 1.75
- pair_gain: float32 [128], replicated, may hold values from 0.25 to 1.75
- w_query: bfloat16 [384, 384], replicated, may hold values from -0.3125 to 0.3125
- w_key: bfloat16 [384, 384], replicated, may hold values from -0.3125 to 0.3125
- w_value: bfloat16 [384, 384], replicated, may hold values from -0.3125 to 0.3125
- w_gate: bfloat16 [384, 384], replicated, may hold values from -0.3125 to 0.3125
- w_bias: bfloat16 [128, 16], replicated, as said below
- chain_penalty: float32 [16], replicated, may hold values from -4 to -0.5
- w_out: bfloat16 [384, 384], replicated, may hold values from -0.3125 to 0.3125
Outputs:
- updated: bfloat16 [2048, 384], P('row', 'col')
The draws below stay inside these ranges and needn't reach their ends.
Inputs may be any that keep to these rules, and one draw needn't show every extreme that they name: `w_bias`: bias weights with standard deviation of order C ** -0.5 or larger.
All inputs are finite; a program needn't handle non-finite values. No bound on the sum of `key_mask` on one device may be relied on, other than what follows from the above.
Results may differ from the reference program's by a relative error of at most 0.0028.
The reference program's roundings to bfloat16 on the way (of `normed`, `query`, `pair_normed` and `gated`) count: a program that leaves them out, or rounds other values in their place, can miss the bound.
Values may be sent and summed in bfloat16 or wider, within the bound.
A program may use at most 64 MiB of HBM per device.

```python
import math
import jax
import jax.numpy as jnp
import numpy as np
from jax import lax

D = 384
HEADS = 16
HEAD = 24
C = 128
QB = 128
TOKENS = 2048
KB = 128
N_ROW = 16
N_COL = 16


def bias_base(key):
    inner = jax.random.fold_in(key, 5)
    return jax.random.normal(inner, (C, HEADS), jnp.float32) / jnp.sqrt(jnp.float32(C))


def draw_w_bias(key, part):
    base = bias_base(key)
    return (base * 2.0).astype(jnp.bfloat16)


def draw_pair(key, part):
    key = jax.random.fold_in(key, 23)
    noise_key = jax.random.fold_in(key, 0)
    noise = jax.random.normal(noise_key, (TOKENS, TOKENS, C), jnp.float32)
    return jnp.clip(noise, -6.0, 6.0).astype(jnp.bfloat16)


def touch_ends(entries, stream_key, smallest, top_value):
    place = [jax.random.randint(jax.random.fold_in(stream_key, axis), (), 0, length) for axis, length in enumerate(entries.shape)]
    longest = entries.shape.index(max(entries.shape))
    next_to = place[:longest] + [(place[longest] + 1) % entries.shape[longest]] + place[longest + 1:]
    return entries.at[tuple(place)].set(smallest).at[tuple(next_to)].set(top_value)


def level_of(own_key, dims, pieces, least, high):
    def one(axis_at, shards_of):
        draws = jax.random.uniform(jax.random.fold_in(jax.random.fold_in(own_key, 6), axis_at), (shards_of,), jnp.float32, least / len(pieces), high / len(pieces))
        return jnp.repeat(jnp.exp(draws), dims[axis_at] // shards_of).reshape((-1,) + (1,) * (len(dims) - axis_at - 1))

    loudness = one(*pieces[0])
    for cut in pieces[1:]:
        loudness = loudness * one(*cut)
    return loudness


def split_up(number_of, total, most, skew):
    loads = [(1 << 20) // math.isqrt(standing ** skew) + 1 for standing in range(2, number_of + 1)]
    surplus, counts = total - most - (number_of - 1), [1] * (number_of - 1)
    while surplus > 0:
        candidates = [i for i in range(number_of - 1) if counts[i] < most]
        whole, budget = sum([loads[i] for i in candidates]), surplus
        for i in candidates:
            more = min(most - counts[i], max(1, budget * loads[i] // whole), surplus)
            counts[i] = counts[i] + more
            surplus = surplus - more
    return np.array([most] + counts)


def ragged_sizes(rng, number_of, total, bound, skew):
    if number_of == 2:
        one = jax.random.randint(rng, (), max(1, total - bound), min(bound, total - 1) + 1)
        return jnp.stack([one, total - one])
    lengths = jnp.asarray(split_up(number_of, total, bound, skew), jnp.int32)
    pairs = (number_of - 1) // 2
    source_of, receiver = lengths[1:1 + 2 * pairs:2], lengths[2:2 + 2 * pairs:2]
    margin = jnp.minimum(source_of - 1, bound - receiver)
    moved = jax.random.randint(jax.random.fold_in(rng, 1), (pairs,), 0, 1 << 20) % (margin + 1)
    lengths = lengths.at[1:1 + 2 * pairs:2].set(source_of - moved).at[2:2 + 2 * pairs:2].set(receiver + moved)
    return lengths[jax.random.permutation(jax.random.fold_in(rng, 2), number_of)]


def centred(own_key, dims, scale, reach, shards=(), kind=jnp.bfloat16):
    drawn = jax.random.normal(own_key, dims, jnp.float32) * scale
    if len(shards) > 0:
        drawn = level_of(own_key, dims, shards, -0.22, 0.18) * drawn
    return jnp.clip(drawn, min=-reach, max=reach).astype(kind)


def setup_inputs(seed: int = 0) -> dict:
    key_list = jax.random.split(jax.random.key(seed), 14)
    return {
        "single": centred(key_list[0], (TOKENS, D), 1.0, 6.0, ((0, 16), (1, 16))),
        "pair": draw_pair(jax.random.fold_in(key_list[13], 71), 0),
        "key_mask": touch_ends((jax.random.randint(key_list[2], (TOKENS,), 0, 8) < 7).astype(jnp.int32), jax.random.fold_in(key_list[2], 1), 0, 1),
        "chain": jnp.searchsorted(jnp.cumsum(ragged_sizes(key_list[3], 8, TOKENS, TOKENS // 4, 1)), jnp.arange(TOKENS), side="right").astype(jnp.int32),
        "single_gain": jnp.clip(1.0 + 0.15 * jax.random.normal(key_list[4], (D,), jnp.float32), 0.25, 1.75),
        "pair_gain": jnp.clip(1.0 + 0.15 * jax.random.normal(key_list[5], (C,), jnp.float32), 0.25, 1.75),
        "w_query": centred(key_list[6], (D, D), D ** -0.5, 0.3125),
        "w_key": centred(key_list[7], (D, D), D ** -0.5, 0.3125),
        "w_value": centred(key_list[8], (D, D), D ** -0.5, 0.3125),
        "w_gate": centred(key_list[9], (D, D), D ** -0.5, 0.3125),
        "w_bias": draw_w_bias(jax.random.fold_in(key_list[13], 71), 0),
        "chain_penalty": jnp.clip(jax.random.uniform(key_list[11], (HEADS,), jnp.float32, -4.0, -0.5), -4.0, -0.5),
        "w_out": centred(key_list[12], (D, D), D ** -0.5, 0.3125),
    }


def norm_last(values, gain):
    mean = lax.optimization_barrier(jnp.mean(values, axis=-1, keepdims=True))
    centered = values - mean
    var = lax.optimization_barrier(jnp.mean(centered * centered, axis=-1, keepdims=True))
    return centered * lax.rsqrt(var + 1e-05) * gain

def reference(single, pair, key_mask, chain, single_gain, pair_gain, w_query, w_key, w_value, w_gate, w_bias, chain_penalty, w_out):
    normed = norm_last(single.astype(jnp.float32), single_gain).astype(jnp.bfloat16)
    query = jnp.dot(normed, w_query, preferred_element_type=jnp.float32).astype(jnp.bfloat16)
    keys = jnp.dot(normed, w_key, preferred_element_type=jnp.float32).astype(jnp.bfloat16)
    values = jnp.dot(normed, w_value, preferred_element_type=jnp.float32).astype(jnp.bfloat16)
    gate = jax.nn.sigmoid(jnp.dot(normed, w_gate, preferred_element_type=jnp.float32))
    keys_h = keys.reshape(TOKENS, HEADS, HEAD).astype(jnp.float32)
    values_b = values.reshape(N_COL, KB, HEADS, HEAD).astype(jnp.float32)
    bias_w = w_bias.astype(jnp.float32)
    valid = key_mask > 0

    def one_block(index):
        start = (index * QB).astype(jnp.int32)
        q_rows = lax.dynamic_slice_in_dim(query, start, QB, 0).reshape(QB, HEADS, HEAD).astype(jnp.float32)
        q_chain = lax.dynamic_slice_in_dim(chain, start, QB, 0)
        tile = lax.dynamic_slice_in_dim(pair, start, QB, 0).astype(jnp.float32)
        pair_normed = norm_last(tile, pair_gain).astype(jnp.bfloat16).astype(jnp.float32)
        bias = jnp.einsum('qkc,ch->hqk', pair_normed, bias_w)
        score = jnp.einsum('qhe,khe->hqk', q_rows, keys_h) / jnp.sqrt(jnp.float32(HEAD)) + bias
        differ = (q_chain[:, None] != chain[None, :]).astype(jnp.float32)
        score = score + chain_penalty[:, None, None] * differ[None]
        score = jnp.where(valid[None, None, :], score, jnp.float32(-1000000000.0))
        score = score.reshape(HEADS, QB, N_COL, KB)
        block_max = lax.optimization_barrier(jnp.max(score, axis=-1))
        expo = jnp.exp(score - block_max[..., None])
        block_total = lax.optimization_barrier(jnp.sum(expo, axis=-1))
        prob = expo.astype(jnp.bfloat16).astype(jnp.float32)
        block_sum = jnp.einsum('hqbk,bkhe->hqbe', prob, values_b)
        top = lax.optimization_barrier(jnp.max(block_max, axis=-1))
        factor = jnp.exp(block_max - top[..., None])
        total = lax.optimization_barrier(jnp.sum(block_total * factor, axis=-1))
        attended = lax.optimization_barrier(jnp.sum(block_sum * factor[..., None], axis=2)) / total[..., None]
        return jnp.transpose(attended, (1, 0, 2)).reshape(QB, D)
    attended = lax.map(one_block, jnp.arange(N_ROW, dtype=jnp.int32)).reshape(TOKENS, D)
    gated = (attended * gate).astype(jnp.bfloat16)
    update = jnp.dot(gated, w_out, preferred_element_type=jnp.float32)
    return (single.astype(jnp.float32) + update).astype(jnp.bfloat16)
```

```python
import functools

import jax
import jax.numpy as jnp
from jax import lax
from jax.experimental import pallas as pl
from jax.experimental.pallas import tpu as pltpu
from jax.sharding import PartitionSpec as P

BF = jnp.bfloat16
F = jnp.float32
MESH = pl.DeviceIdType.MESH
NN = (((1,), (0,)), ((), ()))
NT = (((1,), (1,)), ((), ()))
N = 16
T = 128
D = 384
HEAD = 24
SLOT = 32
C = 128
CHUNKS = 8
CQ = T // CHUNKS
SCALE = 1.0 / 24.0**0.5


def dot(a, b, dims=NN):
    return lax.dot_general(a, b, dims, preferred_element_type=F)


def iota(shape, dim):
    return lax.broadcasted_iota(jnp.int32, shape, dim)


def spread(rows):
    n = rows.shape[1]
    return jnp.concatenate([rows.reshape(N, HEAD, n), jnp.zeros((N, SLOT - HEAD, n), F)], axis=1)


def kernel(
    x_hbm, mask_hbm, chain_hbm, sgain_hbm, pgain_hbm, wb_hbm, pen_hbm,
    wq_hbm, wk_hbm, wv_hbm, wg_hbm, wo_hbm, pair_hbm,
    out_ref,
    x_ref, mask_ref, chain_ref, sgain_ref, pgain_ref, wb_ref, pen_ref,
    pv, bias, w_raw, wq_t, wkv_t, wg_s, wo_s, gain_col, kp, qt, vt,
    piece, recv_a, recv_b, send2, recv2, piece3, recv3,
    in_sem, pair_sem, w_sem, sa, ra, sb, rb, s2, r2, s3, r3,
):
    me_r, me_c = lax.axis_index("row"), lax.axis_index("col")
    diag = me_r == me_c

    def remote(src, dst, send_sem, recv_sem, r, c):
        return pltpu.make_async_remote_copy(
            src_ref=src, dst_ref=dst, send_sem=send_sem, recv_sem=recv_sem,
            device_id=(r, c), device_id_type=MESH,
        )

    def pair_copy(i):
        part = pl.ds(i * CQ, CQ)
        return pltpu.make_async_copy(pair_hbm.at[part], pv.at[part], pair_sem.at[i])

    inputs = [
        pltpu.make_async_copy(src, dst, in_sem.at[i])
        for i, (src, dst) in enumerate(
            (
                (x_hbm, x_ref),
                (mask_hbm, mask_ref),
                (chain_hbm, chain_ref),
                (sgain_hbm, sgain_ref),
                (pgain_hbm, pgain_ref),
                (wb_hbm, wb_ref),
                (pen_hbm, pen_ref),
            )
        )
    ]
    for copy in inputs:
        copy.start()

    barrier = pltpu.get_barrier_semaphore()

    def greet_row(d, _):
        pl.semaphore_signal(
            barrier, inc=1, device_id=(me_r, lax.rem(me_c + d, N)), device_id_type=MESH
        )
        return 0

    def greet_keys(d, _):
        pl.semaphore_signal(
            barrier, inc=1, device_id=(me_c, lax.rem(me_c + d, N)), device_id_type=MESH
        )
        return 0

    lax.fori_loop(1, N, greet_row, 0)
    lax.fori_loop(1, N, greet_keys, 0)

    @pl.when(jnp.logical_not(diag))
    def _():
        pl.semaphore_signal(barrier, inc=1, device_id=(me_c, me_c), device_id_type=MESH)

    for i, w in enumerate((wq_hbm, wk_hbm, wv_hbm, wg_hbm, wo_hbm)):
        pltpu.make_async_copy(w, w_raw.at[i], w_sem.at[i]).start()
    for i in range(CHUNKS):
        pair_copy(i).start()

    for copy in inputs:
        copy.wait()

    x = x_ref[...].astype(F)
    tail_row = iota((SLOT - HEAD, T), 0)
    tail = jnp.where(
        tail_row == 0,
        chain_ref[...].astype(F),
        jnp.where(tail_row == 1, mask_ref[...].astype(F), 0.0),
    )
    mine = jnp.concatenate([x, tail], axis=0).astype(BF)
    piece[...] = mine
    recv_a[me_c] = mine

    pl.semaphore_wait(barrier, 2 * N - 1 - diag.astype(jnp.int32))

    def send_keys(d, _):
        remote(piece, recv_b.at[me_c], sb.at[d], rb.at[me_c], lax.rem(me_r + d, N), me_r).start()
        return 0

    def send_row(d, _):
        remote(piece, recv_a.at[me_c], sa.at[d], ra.at[me_c], me_r, lax.rem(me_c + d, N)).start()
        return 0

    lax.fori_loop(1, N, send_keys, 0)

    @pl.when(jnp.logical_not(diag))
    def _():
        remote(piece, recv_b.at[me_c], sb.at[0], rb.at[me_c], me_r, me_r).start()

    @pl.when(diag)
    def _():
        recv_b[me_c] = mine

    lax.fori_loop(1, N, send_row, 0)

    for i, w in enumerate((wq_hbm, wk_hbm, wv_hbm, wg_hbm, wo_hbm)):
        pltpu.make_async_copy(w, w_raw.at[i], w_sem.at[i]).wait()
    eye_d = (iota((D, D), 0) == iota((D, D), 1)).astype(BF)
    eye_t = (iota((T, T), 0) == iota((T, T), 1)).astype(BF)
    wq_t[...] = dot(eye_d, w_raw[0], NT).astype(BF)
    wkv_t[0:D, :] = dot(eye_d, w_raw[1], NT).astype(BF)
    wkv_t[D : 2 * D, :] = dot(eye_d, w_raw[2], NT).astype(BF)
    own_row = iota((SLOT, D), 0)
    own = ((iota((SLOT, D), 1) == own_row + HEAD * me_c) & (own_row < HEAD)).astype(BF)
    wg_s[...] = dot(own, w_raw[3], NT).astype(BF)
    slot_lane = iota((D, N * SLOT), 1)
    slot_at = lax.rem(slot_lane, SLOT)
    widen = (
        (iota((D, N * SLOT), 0) == (slot_lane // SLOT) * HEAD + slot_at) & (slot_at < HEAD)
    ).astype(BF)
    wo_s[...] = dot(dot(own, w_raw[4], NT).astype(BF), widen).astype(BF)
    for i in range(D // T):
        gain_col[i * T : (i + 1) * T, :] = jnp.broadcast_to(
            sgain_ref[:, i * T : (i + 1) * T], (T, T)
        ).T

    centre = ((iota((C, C), 0) == iota((C, C), 1)).astype(F) - 1.0 / C).astype(BF)
    pgain = pgain_ref[...]
    wb = wb_ref[...]

    def pair_chunk(i, _):
        pair_copy(i).wait()
        tile = pv[pl.ds(i * CQ, CQ)].reshape(CQ * T, C)
        centered = dot(tile, centre)
        var = jnp.mean(centered * centered, axis=-1, keepdims=True)
        normed = (centered * lax.rsqrt(var + 1e-5) * pgain).astype(BF)
        out = dot(wb, normed, NT)
        for u in range(CQ):
            bias[pl.ds(i * CQ + u, N, stride=T), :] = out[:, u * T : (u + 1) * T]
        return 0

    lax.fori_loop(0, CHUNKS, pair_chunk, 0)

    def norm(pieces):
        rows = pieces.astype(F)[:, :HEAD, :].reshape(D, T)
        centered = rows - jnp.mean(rows, axis=0, keepdims=True)
        var = jnp.mean(centered * centered, axis=0, keepdims=True)
        return (centered * lax.rsqrt(var + 1e-5) * gain_col[...]).astype(BF)

    def await_a(d, _):
        s = lax.rem(me_c + d, N)
        remote(piece, recv_a.at[s], sa.at[d], ra.at[s], me_r, s).wait_recv()
        return 0

    def await_b(d, _):
        s = lax.rem(me_c + d, N)
        remote(piece, recv_b.at[s], sb.at[d], rb.at[s], me_c, s).wait_recv()
        return 0

    lax.fori_loop(1, N, await_a, 0)
    normed_q = norm(recv_a[...])
    qt[...] = spread(dot(wq_t[...], normed_q)).astype(BF)
    gate = jax.nn.sigmoid(dot(wg_s[...], normed_q))

    lax.fori_loop(1, N, await_b, 0)

    @pl.when(jnp.logical_not(diag))
    def _():
        remote(piece, recv_b.at[me_c], sb.at[0], rb.at[me_c], me_c, me_c).wait_recv()

    both = dot(wkv_t[...], norm(recv_b[...]))
    vt[...] = spread(both[D:]).astype(BF)
    keys = dot(eye_t, spread(both[:D]).astype(BF).reshape(N * SLOT, T), NT).astype(BF)
    for b in range(4):
        kp[b] = keys[:, b * T : (b + 1) * T]

    info = recv_b[0].astype(F)
    chain_k = jnp.broadcast_to(info[HEAD : HEAD + 1], (T, T)).T
    valid = jnp.broadcast_to(info[HEAD + 1 : HEAD + 2], (T, T)).T > 0.5
    differ = (chain_k != chain_ref[...].astype(F)).astype(F)
    stat_row = iota((SLOT - HEAD, T), 0)
    zeros = jnp.zeros((SLOT, T), BF)

    def head_group(t, _):
        b = lax.rem(me_c // 4 + 1 + t, 4)
        blocks = [
            jnp.concatenate([qt[b * 4 + j] if i == j else zeros for i in range(4)], axis=0)
            for j in range(4)
        ]
        scores = dot(kp[b], jnp.concatenate(blocks, axis=1))
        for j in range(4):
            h = b * 4 + j
            pair_bias = bias[pl.ds(pl.multiple_of(h * T, T), T), :].T
            score = scores[:, j * T : (j + 1) * T] * SCALE + pair_bias + pen_ref[0, h] * differ
            score = jnp.where(valid, score, -1e9)
            top = jnp.max(score, axis=0, keepdims=True)
            expo = jnp.exp(score - top)
            total = jnp.sum(expo, axis=0, keepdims=True)
            weighted = dot(vt[h], expo.astype(BF))
            stats = jnp.where(stat_row == 0, top, jnp.where(stat_row == 1, total, 0.0))
            send2[h] = jnp.concatenate([weighted[:HEAD], stats], axis=0)

            @pl.when(h != me_c)
            def _():
                remote(send2.at[h], recv2.at[me_c], s2.at[h], r2.at[me_c], me_r, h).start()

            @pl.when(h == me_c)
            def _():
                recv2[me_c] = send2[h]

        return 0

    lax.fori_loop(0, 4, head_group, 0)

    def await_2(d, _):
        s = lax.rem(me_c + d, N)
        remote(send2.at[s], recv2.at[s], s2.at[s], r2.at[s], me_r, s).wait_recv()
        return 0

    lax.fori_loop(1, N, await_2, 0)
    tops = recv2[:, HEAD : HEAD + 1, :]
    top = jnp.max(tops, axis=0, keepdims=True)
    factor = jnp.exp(tops - top)
    total = jnp.sum(recv2[:, HEAD + 1 : HEAD + 2, :] * factor, axis=0)
    summed = jnp.sum(recv2[:, :HEAD, :] * factor, axis=0)
    gated = summed / total * gate[:HEAD]
    gated = jnp.concatenate([gated, jnp.zeros((SLOT - HEAD, T), F)], axis=0).astype(BF)
    piece3[...] = gated
    recv3[me_c] = gated

    def send_gated(d, _):
        c = lax.rem(me_c + d, N)
        remote(piece3, recv3.at[me_c], s3.at[d], r3.at[me_c], me_r, c).start()
        return 0

    def await_3(d, _):
        s = lax.rem(me_c + d, N)
        remote(piece3, recv3.at[s], s3.at[d], r3.at[s], me_r, s).wait_recv()
        return 0

    lax.fori_loop(1, N, send_gated, 0)
    lax.fori_loop(1, N, await_3, 0)
    update = dot(wo_s[...], recv3[...].reshape(N * SLOT, T))
    out_ref[...] = (x + update[:HEAD]).astype(BF)

    def sent(d, _):
        s = lax.rem(me_c + d, N)
        remote(piece, recv_a.at[me_c], sa.at[d], ra.at[me_c], me_r, s).wait_send()
        remote(piece, recv_b.at[me_c], sb.at[d], rb.at[me_c], me_r, s).wait_send()
        remote(send2.at[s], recv2.at[me_c], s2.at[s], r2.at[me_c], me_r, s).wait_send()
        remote(piece3, recv3.at[me_c], s3.at[d], r3.at[me_c], me_r, s).wait_send()
        return 0

    lax.fori_loop(1, N, sent, 0)

    @pl.when(jnp.logical_not(diag))
    def _():
        remote(piece, recv_b.at[me_c], sb.at[0], rb.at[me_c], me_r, me_r).wait_send()


def per_device(
    single, pair, key_mask, chain, single_gain, pair_gain,
    w_query, w_key, w_value, w_gate, w_bias, chain_penalty, w_out,
):
    vmem = pl.BlockSpec(memory_space=pltpu.VMEM)
    hbm = pl.BlockSpec(memory_space=pltpu.HBM)
    sems = pltpu.SemaphoreType.DMA((N,))
    out = pl.pallas_call(
        kernel,
        out_shape=jax.ShapeDtypeStruct((HEAD, T), BF),
        in_specs=[hbm] * 13,
        out_specs=vmem,
        scratch_shapes=[
            pltpu.VMEM((HEAD, T), BF),
            pltpu.VMEM((1, T), jnp.int32),
            pltpu.VMEM((1, T), jnp.int32),
            pltpu.VMEM((1, D), F),
            pltpu.VMEM((1, C), F),
            pltpu.VMEM((N, C), BF),
            pltpu.SMEM((1, N), F),
            pltpu.VMEM((T, T, C), BF),
            pltpu.VMEM((N * T, T), F),
            pltpu.VMEM((5, D, D), BF),
            pltpu.VMEM((D, D), BF),
            pltpu.VMEM((2 * D, D), BF),
            pltpu.VMEM((SLOT, D), BF),
            pltpu.VMEM((SLOT, N * SLOT), BF),
            pltpu.VMEM((D, T), F),
            pltpu.VMEM((4, T, T), BF),
            pltpu.VMEM((N, SLOT, T), BF),
            pltpu.VMEM((N, SLOT, T), BF),
            pltpu.VMEM((SLOT, T), BF),
            pltpu.VMEM((N, SLOT, T), BF),
            pltpu.VMEM((N, SLOT, T), BF),
            pltpu.VMEM((N, SLOT, T), F),
            pltpu.VMEM((N, SLOT, T), F),
            pltpu.VMEM((SLOT, T), BF),
            pltpu.VMEM((N, SLOT, T), BF),
            pltpu.SemaphoreType.DMA((7,)),
            pltpu.SemaphoreType.DMA((CHUNKS,)),
            pltpu.SemaphoreType.DMA((5,)),
        ]
        + [sems] * 8,
        compiler_params=pltpu.CompilerParams(
            collective_id=0, has_side_effects=True, vmem_limit_bytes=56 << 20
        ),
        name="pair_attention",
    )(
        single.T, key_mask.reshape(1, T), chain.reshape(1, T), single_gain.reshape(1, D),
        pair_gain.reshape(1, C), w_bias.T, chain_penalty.reshape(1, N),
        w_query, w_key, w_value, w_gate, w_out, pair,
    )
    return out.T


def solution(mesh):
    placed = (P("row", "col"), P("row", "col", None), P("row"), P("row")) + (P(),) * 9
    return jax.shard_map(
        per_device, mesh=mesh, in_specs=placed, out_specs=P("row", "col"), check_vma=False
    )
```

```python
import functools

import jax
import jax.numpy as jnp
from jax import lax
from jax.experimental import pallas as pl
from jax.experimental.pallas import tpu as pltpu
from jax.sharding import PartitionSpec as P

BF = jnp.bfloat16
F = jnp.float32
MESH = pl.DeviceIdType.MESH
NN = (((1,), (0,)), ((), ()))
NT = (((1,), (1,)), ((), ()))
N = 16
T = 128
D = 384
HEAD = 24
SLOT = 32
C = 128
CHUNKS = 8
CQ = T // CHUNKS
SCALE = 1.0 / 24.0**0.5


def dot(a, b, dims=NN):
    return lax.dot_general(a, b, dims, preferred_element_type=F)


def iota(shape, dim):
    return lax.broadcasted_iota(jnp.int32, shape, dim)


def spread(rows):
    n = rows.shape[1]
    return jnp.concatenate([rows.reshape(N, HEAD, n), jnp.zeros((N, SLOT - HEAD, n), F)], axis=1)


def kernel(
    x_hbm, mask_hbm, chain_hbm, sgain_hbm, pgain_hbm, wb_hbm, pen_hbm,
    wq_hbm, wk_hbm, wv_hbm, wg_hbm, wo_hbm, pair_hbm,
    out_ref,
    x_ref, mask_ref, chain_ref, sgain_ref, pgain_ref, wb_ref, pen_ref,
    pv, bias, bias_t, w_raw, wq_t, wkv_t, wg_s, wo_s, gain_col, kp, qt, vt,
    piece, recv_a, recv_b, send2, recv2, piece3, recv3,
    in_sem, pair_sem, w_sem, sa, ra, sb, rb, sf, rf, s2, r2, s3, r3,
):
    me_r, me_c = lax.axis_index("row"), lax.axis_index("col")
    diag = me_r == me_c
    core, side = lax.rem(me_r, 2), lax.rem(me_c, 2)
    sibling = me_r + 1 - 2 * core
    others = pl.ds(0, N - 1)

    def remote(src, dst, send_sem, recv_sem, r, c):
        return pltpu.make_async_remote_copy(
            src_ref=src, dst_ref=dst, send_sem=send_sem, recv_sem=recv_sem,
            device_id=(r, c), device_id_type=MESH,
        )

    def pair_copy(i):
        part = pl.ds(i * CQ, CQ)
        return pltpu.make_async_copy(pair_hbm.at[part], pv.at[part], pair_sem.at[i])

    inputs = [
        pltpu.make_async_copy(src, dst, in_sem.at[i])
        for i, (src, dst) in enumerate(
            (
                (x_hbm, x_ref),
                (mask_hbm, mask_ref.at[0]),
                (chain_hbm, chain_ref.at[0]),
                (sgain_hbm, sgain_ref.at[0]),
                (pgain_hbm, pgain_ref.at[0]),
                (wb_hbm, wb_ref),
                (pen_hbm, pen_ref),
            )
        )
    ]
    for copy in inputs:
        copy.start()

    barrier = pltpu.get_barrier_semaphore()

    def greet_row(d, _):
        pl.semaphore_signal(
            barrier, inc=1, device_id=(me_r, lax.rem(me_c + d, N)), device_id_type=MESH
        )
        return 0

    def greet_keys(m, _):
        pl.semaphore_signal(
            barrier,
            inc=1,
            device_id=(me_c, 2 * lax.rem(me_r // 2 + m, N // 2) + core),
            device_id_type=MESH,
        )
        return 0

    lax.fori_loop(1, N // 2, greet_keys, 0)

    @pl.when(jnp.logical_not(diag))
    def _():
        greet_keys(0, 0)

    pl.semaphore_signal(barrier, inc=1, device_id=(sibling, me_c), device_id_type=MESH)
    lax.fori_loop(1, N, greet_row, 0)

    for i, w in enumerate((wq_hbm, wk_hbm, wv_hbm, wg_hbm, wo_hbm)):
        pltpu.make_async_copy(w, w_raw.at[i], w_sem).start()
    for i in range(CHUNKS):
        pair_copy(i).start()

    for copy in inputs:
        copy.wait()

    x = x_ref[...].astype(F)
    tail_row = iota((SLOT - HEAD, T), 0)
    tail = jnp.where(
        tail_row == 0,
        chain_ref[...].astype(F),
        jnp.where(tail_row == 1, mask_ref[...].astype(F), 0.0),
    )
    mine = jnp.concatenate([x, tail], axis=0).astype(BF)
    piece[...] = mine
    recv_a[me_c] = mine

    pl.semaphore_wait(barrier, N - 1 + N // 2 + 1 - diag.astype(jnp.int32))

    def send_keys(m, _):
        r = 2 * lax.rem(me_r // 2 + m, N // 2) + side
        remote(piece, recv_b.at[side, me_c // 2], sb, rb, r, me_r).start()
        return 0

    def send_row(d, _):
        remote(piece, recv_a.at[me_c], sa, ra, me_r, lax.rem(me_c + d, N)).start()
        return 0

    lax.fori_loop(1, N // 2, send_keys, 0)

    @pl.when(jnp.logical_not(diag))
    def _():
        send_keys(0, 0)

    @pl.when(diag)
    def _():
        recv_b[side, me_c // 2] = mine

    lax.fori_loop(1, N, send_row, 0)

    pltpu.make_async_copy(w_raw, w_raw, w_sem).wait()
    eye_d = (iota((D, D), 0) == iota((D, D), 1)).astype(BF)
    eye_t = (iota((T, T), 0) == iota((T, T), 1)).astype(BF)
    wq_t[...] = dot(eye_d, w_raw[0], NT).astype(BF)
    wkv_t[0:D, :] = dot(eye_d, w_raw[1], NT).astype(BF)
    wkv_t[D : 2 * D, :] = dot(eye_d, w_raw[2], NT).astype(BF)
    own_row = iota((SLOT, D), 0)
    own = ((iota((SLOT, D), 1) == own_row + HEAD * me_c) & (own_row < HEAD)).astype(BF)
    wg_s[...] = dot(own, w_raw[3], NT).astype(BF)
    slot_lane = iota((D, N * SLOT), 1)
    slot_at = lax.rem(slot_lane, SLOT)
    widen = (
        (iota((D, N * SLOT), 0) == (slot_lane // SLOT) * HEAD + slot_at) & (slot_at < HEAD)
    ).astype(BF)
    wo_s[...] = dot(dot(own, w_raw[4], NT).astype(BF), widen).astype(BF)
    for i in range(D // T):
        gain_col[i * T : (i + 1) * T, :] = jnp.broadcast_to(
            sgain_ref[:, i * T : (i + 1) * T], (T, T)
        ).T

    centre = ((iota((C, C), 0) == iota((C, C), 1)).astype(F) - 1.0 / C).astype(BF)
    pgain = pgain_ref[...]
    wb = wb_ref[...]

    def pair_chunk(i, _):
        pair_copy(i).wait()
        tile = pv[pl.ds(i * CQ, CQ)].reshape(CQ * T, C)
        centered = dot(tile, centre)
        var = jnp.mean(centered * centered, axis=-1, keepdims=True)
        normed = (centered * lax.rsqrt(var + 1e-5) * pgain).astype(BF)
        out = dot(wb, normed, NT)
        for u in range(CQ):
            bias[pl.ds(i * CQ + u, N, stride=T), :] = out[:, u * T : (u + 1) * T]
        return 0

    lax.fori_loop(0, CHUNKS - 2, pair_chunk, 0)

    direct = recv_b.at[core]

    @pl.when(diag)
    def _():
        some = recv_b.at[core, pl.ds(0, N // 2 - 1)]
        remote(some, some, sb, rb, sibling, me_c).wait_recv()

    @pl.when(jnp.logical_not(diag))
    def _():
        remote(direct, direct, sb, rb, sibling, me_c).wait_recv()

    forward = remote(direct, direct, sf, rf, sibling, me_c)
    forward.start()
    lax.fori_loop(CHUNKS - 2, CHUNKS, pair_chunk, 0)

    def turn(b, _):
        for j in range(4):
            rows = pl.ds(pl.multiple_of((b * 4 + j) * T, T), T)
            bias_t[b, :, j * T : (j + 1) * T] = bias[rows, :].T
        return 0

    lax.fori_loop(0, 4, turn, 0)

    def norm(pieces):
        rows = jnp.concatenate([part.astype(F)[:HEAD] for part in pieces], axis=0)
        centered = rows - jnp.mean(rows, axis=0, keepdims=True)
        var = jnp.mean(centered * centered, axis=0, keepdims=True)
        return (centered * lax.rsqrt(var + 1e-5) * gain_col[...]).astype(BF)

    remote(recv_a.at[others], recv_a.at[others], sa, ra, me_r, me_c).wait_recv()
    normed_q = norm([recv_a[s] for s in range(N)])
    qt[...] = spread(dot(wq_t[...], normed_q)).astype(BF)
    gate = jax.nn.sigmoid(dot(wg_s[...], normed_q))

    remote(recv_b.at[1 - core], recv_b.at[1 - core], sf, rf, sibling, me_c).wait_recv()
    both = dot(wkv_t[...], norm([recv_b[s % 2, s // 2] for s in range(N)]))
    vt[...] = spread(both[D:]).astype(BF).reshape(4, 4 * SLOT, T)
    keys = dot(eye_t, spread(both[:D]).astype(BF).reshape(N * SLOT, T), NT).astype(BF)
    for b in range(4):
        kp[b] = keys[:, b * T : (b + 1) * T]

    info = recv_b[0, 0].astype(F)
    chain_k = jnp.broadcast_to(info[HEAD : HEAD + 1], (T, T)).T
    mask_k = jnp.broadcast_to(info[HEAD + 1 : HEAD + 2], (T, T)).T
    valid = jnp.concatenate([mask_k] * 4, axis=1) > 0.5
    differ = (chain_k != chain_ref[...].astype(F)).astype(F)
    stat_row = iota((SLOT - HEAD, 4 * T), 0)
    zeros = jnp.zeros((SLOT, T), BF)

    z_hi, z_lo = me_c // 8, lax.rem(me_c // 4, 2)

    def head_group(t, _):
        far = 1 - t // 2
        b = 2 * lax.rem(z_hi + far, 2) + lax.rem(z_lo + t + t // 2, 2)
        blocks = [
            jnp.concatenate([qt[b * 4 + j] if i == j else zeros for i in range(4)], axis=0)
            for j in range(4)
        ]
        raw = dot(kp[b], jnp.concatenate(blocks, axis=1))
        chains = jnp.concatenate([pen_ref[b * 4 + j] * differ for j in range(4)], axis=1)
        score = raw * SCALE + bias_t[b] + chains
        score = jnp.where(valid, score, -1e9)
        top = jnp.max(score, axis=0, keepdims=True)
        expo = jnp.exp(score - top)
        total = jnp.sum(expo, axis=0, keepdims=True)
        weighted = dot(vt[b], expo.astype(BF))
        stats = jnp.where(stat_row == 0, top, jnp.where(stat_row == 1, total, 0.0))
        for j in range(4):
            lanes = slice(j * T, (j + 1) * T)
            send2[b * 4 + j] = jnp.concatenate(
                [weighted[j * SLOT : j * SLOT + HEAD, lanes], stats[:, lanes]], axis=0
            )
        for j in range(4):
            h = b * 4 + j

            @pl.when(h != me_c)
            def _():
                remote(send2.at[h], recv2.at[me_c], s2, r2, me_r, h).start()

            @pl.when(h == me_c)
            def _():
                recv2[me_c] = send2[h]

        return 0

    lax.fori_loop(0, 4, head_group, 0)

    remote(send2.at[others], recv2.at[others], s2, r2, me_r, me_c).wait_recv()
    tops = recv2[:, HEAD : HEAD + 1, :]
    top = jnp.max(tops, axis=0, keepdims=True)
    factor = jnp.exp(tops - top)
    total = jnp.sum(recv2[:, HEAD + 1 : HEAD + 2, :] * factor, axis=0)
    summed = jnp.sum(recv2[:, :HEAD, :] * factor, axis=0)
    gated = summed / total * gate[:HEAD]
    gated = jnp.concatenate([gated, jnp.zeros((SLOT - HEAD, T), F)], axis=0).astype(BF)
    piece3[...] = gated
    recv3[me_c] = gated

    def send_gated(d, _):
        c = lax.rem(me_c + d, N)
        remote(piece3, recv3.at[me_c], s3, r3, me_r, c).start()
        return 0

    lax.fori_loop(1, N, send_gated, 0)
    remote(recv3.at[others], recv3.at[others], s3, r3, me_r, me_c).wait_recv()
    update = dot(wo_s[...], recv3[...].reshape(N * SLOT, T))
    out_ref[...] = (x + update[:HEAD]).astype(BF)

    forward.wait_send()
    remote(recv_a.at[others], recv_a.at[others], sa, ra, me_r, me_c).wait_send()
    remote(send2.at[others], recv2.at[others], s2, r2, me_r, me_c).wait_send()
    remote(recv3.at[others], recv3.at[others], s3, r3, me_r, me_c).wait_send()

    @pl.when(diag)
    def _():
        some = recv_b.at[core, pl.ds(0, N // 2 - 1)]
        remote(some, some, sb, rb, sibling, me_c).wait_send()

    @pl.when(jnp.logical_not(diag))
    def _():
        remote(direct, direct, sb, rb, sibling, me_c).wait_send()


def per_device(
    single, pair, key_mask, chain, single_gain, pair_gain,
    w_query, w_key, w_value, w_gate, w_bias, chain_penalty, w_out,
):
    vmem = pl.BlockSpec(memory_space=pltpu.VMEM)
    hbm = pl.BlockSpec(memory_space=pltpu.HBM)
    out = pl.pallas_call(
        kernel,
        out_shape=pltpu.VMEM((HEAD, T), BF),
        in_specs=[hbm] * 13,
        out_specs=vmem,
        scratch_shapes=[
            pltpu.VMEM((HEAD, T), BF),
            pltpu.VMEM((1, T), jnp.int32),
            pltpu.VMEM((1, T), jnp.int32),
            pltpu.VMEM((1, D), F),
            pltpu.VMEM((1, C), F),
            pltpu.VMEM((N, C), BF),
            pltpu.SMEM((N,), F),
            pltpu.VMEM((T, T, C), BF),
            pltpu.VMEM((N * T, T), F),
            pltpu.VMEM((4, T, 4 * T), F),
            pltpu.VMEM((5, D, D), BF),
            pltpu.VMEM((D, D), BF),
            pltpu.VMEM((2 * D, D), BF),
            pltpu.VMEM((SLOT, D), BF),
            pltpu.VMEM((SLOT, N * SLOT), BF),
            pltpu.VMEM((D, T), F),
            pltpu.VMEM((4, T, T), BF),
            pltpu.VMEM((N, SLOT, T), BF),
            pltpu.VMEM((4, 4 * SLOT, T), BF),
            pltpu.VMEM((SLOT, T), BF),
            pltpu.VMEM((N, SLOT, T), BF),
            pltpu.VMEM((2, N // 2, SLOT, T), BF),
            pltpu.VMEM((N, SLOT, T), F),
            pltpu.VMEM((N, SLOT, T), F),
            pltpu.VMEM((SLOT, T), BF),
            pltpu.VMEM((N, SLOT, T), BF),
            pltpu.SemaphoreType.DMA((7,)),
            pltpu.SemaphoreType.DMA((CHUNKS,)),
        ]
        + [pltpu.SemaphoreType.DMA] * 11,
        compiler_params=pltpu.CompilerParams(
            collective_id=0, has_side_effects=True, vmem_limit_bytes=56 << 20
        ),
        name="pair_attention",
    )(
        single.T, key_mask, chain, single_gain, pair_gain, w_bias.T, chain_penalty,
        w_query, w_key, w_value, w_gate, w_out, pair,
    )
    return out.T


def solution(mesh):
    placed = (P("row", "col"), P("row", "col", None), P("row"), P("row")) + (P(),) * 9
    return jax.shard_map(
        per_device, mesh=mesh, in_specs=placed, out_specs=P("row", "col"), check_vma=False
    )
```

```python
import functools

import jax
import jax.numpy as jnp
from jax import lax
from jax.experimental import pallas as pl
from jax.experimental.pallas import tpu as pltpu
from jax.sharding import PartitionSpec as P

BF = jnp.bfloat16
F = jnp.float32
MESH = pl.DeviceIdType.MESH
NN = (((1,), (0,)), ((), ()))
NT = (((1,), (1,)), ((), ()))
N = 16
T = 128
D = 384
HEAD = 24
SLOT = 32
C = 128
CHUNKS = 4
CQ = T // CHUNKS
EARLY = 2
SCALE = 1.0 / 24.0**0.5


def dot(a, b, dims=NN):
    return lax.dot_general(a, b, dims, preferred_element_type=F)


def iota(shape, dim):
    return lax.broadcasted_iota(jnp.int32, shape, dim)


def spread(rows):
    n = rows.shape[1]
    return jnp.concatenate([rows.reshape(N, HEAD, n), jnp.zeros((N, SLOT - HEAD, n), F)], axis=1)


def kernel(
    x_hbm, mask_hbm, chain_hbm, sgain_hbm, pgain_hbm, wb_hbm, pen_hbm,
    wq_hbm, wk_hbm, wv_hbm, wg_hbm, wo_hbm, pair_hbm,
    out_ref,
    x_ref, mask_ref, chain_ref, sgain_ref, pgain_ref, wb_ref, pen_ref,
    pv, bias, bias_t, w_raw, wq_t, wkv_t, wg_s, wo_s, gain_col, kp, qt, vt,
    piece, recv_a, recv_b, send2, recv2, piece3, recv3,
    in_sem, pair_sem, w_sem, sa, ra, sx, rx, sb, rb, sf, rf, s2, r2, s3, r3,
):
    me_r, me_c = lax.axis_index("row"), lax.axis_index("col")
    diag = me_r == me_c
    core, side = lax.rem(me_r, 2), lax.rem(me_c, 2)
    sibling = me_r + 1 - 2 * core
    others, three = pl.ds(0, N - 1), pl.ds(0, 3)
    at_z, at_x = me_c // 4, lax.rem(me_c, 4)

    def along_z(d):
        return lax.rem(at_z + d, 4) * 4 + at_x

    def along_x(d):
        return at_z * 4 + lax.rem(at_x + d, 4)

    def remote(src, dst, send_sem, recv_sem, r, c):
        return pltpu.make_async_remote_copy(
            src_ref=src, dst_ref=dst, send_sem=send_sem, recv_sem=recv_sem,
            device_id=(r, c), device_id_type=MESH,
        )

    def pair_copy(i):
        part = pl.ds(i * CQ, CQ)
        return pltpu.make_async_copy(pair_hbm.at[part], pv.at[part], pair_sem.at[i])

    inputs = [
        pltpu.make_async_copy(src, dst, in_sem.at[i])
        for i, (src, dst) in enumerate(
            (
                (x_hbm, x_ref),
                (mask_hbm, mask_ref.at[0]),
                (chain_hbm, chain_ref.at[0]),
                (sgain_hbm, sgain_ref.at[0]),
                (pgain_hbm, pgain_ref.at[0]),
                (wb_hbm, wb_ref),
                (pen_hbm, pen_ref),
            )
        )
    ]
    for copy in inputs[:3]:
        copy.start()

    barrier = pltpu.get_barrier_semaphore()

    def greet_keys(m, _):
        pl.semaphore_signal(
            barrier,
            inc=1,
            device_id=(me_c, 2 * lax.rem(me_r // 2 + m, N // 2) + core),
            device_id_type=MESH,
        )
        return 0

    lax.fori_loop(1, N // 2, greet_keys, 0)

    @pl.when(jnp.logical_not(diag))
    def _():
        greet_keys(0, 0)

    pl.semaphore_signal(barrier, inc=1, device_id=(sibling, me_c), device_id_type=MESH)
    for d in (1, 2, 3):
        for c in (along_z(d), along_x(d)):
            pl.semaphore_signal(barrier, inc=1, device_id=(me_r, c), device_id_type=MESH)

    for copy in inputs[3:]:
        copy.start()
    for i, w in enumerate((wq_hbm, wk_hbm, wv_hbm, wg_hbm, wo_hbm)):
        pltpu.make_async_copy(w, w_raw.at[i], w_sem).start()
    for i in range(CHUNKS):
        pair_copy(i).start()

    for copy in inputs[:3]:
        copy.wait()

    x = x_ref[...].astype(F)
    tail_row = iota((SLOT - HEAD, T), 0)
    tail = jnp.where(
        tail_row == 0,
        chain_ref[...].astype(F),
        jnp.where(tail_row == 1, mask_ref[...].astype(F), 0.0),
    )
    mine = jnp.concatenate([x, tail], axis=0).astype(BF)
    piece[...] = mine
    recv_a[at_x, at_z] = mine

    pl.semaphore_wait(barrier, 6 + N // 2 + 1 - diag.astype(jnp.int32))

    def send_keys(m, _):
        r = 2 * lax.rem(me_r // 2 + m, N // 2) + side
        remote(piece, recv_b.at[side, me_c // 2], sb, rb, r, me_r).start()
        return 0

    for d in (1, 2, 3):
        remote(piece, recv_a.at[at_x, at_z], sa, ra, me_r, along_z(d)).start()

    lax.fori_loop(1, N // 2, send_keys, 0)

    @pl.when(jnp.logical_not(diag))
    def _():
        send_keys(0, 0)

    @pl.when(diag)
    def _():
        recv_b[side, me_c // 2] = mine

    for copy in inputs[3:]:
        copy.wait()

    pltpu.make_async_copy(w_raw, w_raw, w_sem).wait()
    eye_d = (iota((D, D), 0) == iota((D, D), 1)).astype(BF)
    eye_t = (iota((T, T), 0) == iota((T, T), 1)).astype(BF)
    wq_t[...] = dot(eye_d, w_raw[0], NT).astype(BF)
    wkv_t[0:D, :] = dot(eye_d, w_raw[1], NT).astype(BF)
    wkv_t[D : 2 * D, :] = dot(eye_d, w_raw[2], NT).astype(BF)
    own_row = iota((SLOT, D), 0)
    own = ((iota((SLOT, D), 1) == own_row + HEAD * me_c) & (own_row < HEAD)).astype(BF)
    wg_s[...] = dot(own, w_raw[3], NT).astype(BF)
    slot_lane = iota((D, N * SLOT), 1)
    slot_at = lax.rem(slot_lane, SLOT)
    widen = (
        (iota((D, N * SLOT), 0) == (slot_lane // SLOT) * HEAD + slot_at) & (slot_at < HEAD)
    ).astype(BF)
    wo_s[...] = dot(dot(own, w_raw[4], NT).astype(BF), widen).astype(BF)
    for i in range(D // T):
        gain_col[i * T : (i + 1) * T, :] = jnp.broadcast_to(
            sgain_ref[:, i * T : (i + 1) * T], (T, T)
        ).T

    centre = ((iota((C, C), 0) == iota((C, C), 1)).astype(F) - 1.0 / C).astype(BF)
    pgain = pgain_ref[...]
    wb = wb_ref[...]

    def pair_chunk(i, _):
        pair_copy(i).wait()
        tile = pv[pl.ds(i * CQ, CQ)].reshape(CQ * T, C)
        centered = dot(tile, centre)
        var = jnp.mean(centered * centered, axis=-1, keepdims=True)
        normed = (centered * lax.rsqrt(var + 1e-5) * pgain).astype(BF)
        out = dot(wb, normed, NT)
        for u in range(CQ):
            bias[pl.ds(i * CQ + u, N, stride=T), :] = out[:, u * T : (u + 1) * T]
        return 0

    direct = recv_b.at[core]
    forward = remote(direct, direct, sf, rf, sibling, me_c)
    column, columns = recv_a.at[at_x], recv_a.at[three]

    def pair_step(i, _):
        @pl.when(i == EARLY)
        def _():
            remote(recv_a.at[0, three], recv_a.at[0, three], sa, ra, me_r, me_c).wait_recv()
            for d in (1, 2, 3):
                remote(column, column, sx, rx, me_r, along_x(d)).start()

        return pair_chunk(i, 0)

    lax.fori_loop(0, CHUNKS, pair_step, 0)

    @pl.when(diag)
    def _():
        some = recv_b.at[core, pl.ds(0, N // 2 - 1)]
        remote(some, some, sb, rb, sibling, me_c).wait_recv()

    @pl.when(jnp.logical_not(diag))
    def _():
        remote(direct, direct, sb, rb, sibling, me_c).wait_recv()

    forward.start()

    def turn(b, _):
        for j in range(4):
            rows = pl.ds(pl.multiple_of((b * 4 + j) * T, T), T)
            bias_t[b, :, j * T : (j + 1) * T] = bias[rows, :].T
        return 0

    lax.fori_loop(0, 4, turn, 0)

    def norm(pieces):
        rows = jnp.concatenate([part.astype(F)[:HEAD] for part in pieces], axis=0)
        centered = rows - jnp.mean(rows, axis=0, keepdims=True)
        var = jnp.mean(centered * centered, axis=0, keepdims=True)
        return (centered * lax.rsqrt(var + 1e-5) * gain_col[...]).astype(BF)

    remote(columns, columns, sx, rx, me_r, me_c).wait_recv()
    normed_q = norm([recv_a[s % 4, s // 4] for s in range(N)])
    qt[...] = spread(dot(wq_t[...], normed_q)).astype(BF)
    gate = jax.nn.sigmoid(dot(wg_s[...], normed_q))

    remote(recv_b.at[1 - core], recv_b.at[1 - core], sf, rf, sibling, me_c).wait_recv()
    both = dot(wkv_t[...], norm([recv_b[s % 2, s // 2] for s in range(N)]))
    vt[...] = spread(both[D:]).astype(BF).reshape(4, 4 * SLOT, T)
    keys = dot(eye_t, spread(both[:D]).astype(BF).reshape(N * SLOT, T), NT).astype(BF)
    for b in range(4):
        kp[b] = keys[:, b * T : (b + 1) * T]

    info = recv_b[0, 0].astype(F)
    chain_k = jnp.broadcast_to(info[HEAD : HEAD + 1], (T, T)).T
    mask_k = jnp.broadcast_to(info[HEAD + 1 : HEAD + 2], (T, T)).T
    valid = jnp.concatenate([mask_k] * 4, axis=1) > 0.5
    differ = (chain_k != chain_ref[...].astype(F)).astype(F)
    stat_row = iota((SLOT - HEAD, 4 * T), 0)
    zeros = jnp.zeros((SLOT, T), BF)

    z_hi, z_lo = me_c // 8, lax.rem(me_c // 4, 2)

    def head_group(t, _):
        far = 1 - t // 2
        b = 2 * lax.rem(z_hi + far, 2) + lax.rem(z_lo + t + t // 2, 2)
        blocks = [
            jnp.concatenate([qt[b * 4 + j] if i == j else zeros for i in range(4)], axis=0)
            for j in range(4)
        ]
        raw = dot(kp[b], jnp.concatenate(blocks, axis=1))
        chains = jnp.concatenate([pen_ref[b * 4 + j] * differ for j in range(4)], axis=1)
        score = raw * SCALE + bias_t[b] + chains
        score = jnp.where(valid, score, -1e9)
        top = jnp.max(score, axis=0, keepdims=True)
        expo = jnp.exp(score - top)
        total = jnp.sum(expo, axis=0, keepdims=True)
        weighted = dot(vt[b], expo.astype(BF))
        stats = jnp.where(stat_row == 0, top, jnp.where(stat_row == 1, total, 0.0))
        for j in range(4):
            lanes = slice(j * T, (j + 1) * T)
            sums = weighted[j * SLOT : j * SLOT + HEAD, lanes]
            send2[b * 4 + j, : HEAD // 2] = sums.reshape(HEAD // 2, 2, T)
            send2[b * 4 + j, HEAD // 2] = stats[:2, lanes]
        for j in range(4):
            h = b * 4 + j

            @pl.when(h != me_c)
            def _():
                remote(send2.at[h], recv2.at[me_c], s2, r2, me_r, h).start()

            @pl.when(h == me_c)
            def _():
                recv2[me_c] = send2[h]

        return 0

    lax.fori_loop(0, 4, head_group, 0)

    remote(send2.at[others], recv2.at[others], s2, r2, me_r, me_c).wait_recv()
    stats = recv2[:, HEAD // 2]
    tops = stats[:, 0:1]
    top = jnp.max(tops, axis=0, keepdims=True)
    factor = jnp.exp(tops - top)
    total = jnp.sum(stats[:, 1:2] * factor, axis=0)
    summed = jnp.sum(recv2[:, : HEAD // 2] * factor[:, :, None], axis=0).reshape(HEAD, T)
    gated = summed / total * gate[:HEAD]
    gated = jnp.concatenate([gated, jnp.zeros((SLOT - HEAD, T), F)], axis=0).astype(BF)
    piece3[...] = gated
    recv3[me_c] = gated

    def send_gated(d, _):
        c = lax.rem(me_c + d, N)
        remote(piece3, recv3.at[me_c], s3, r3, me_r, c).start()
        return 0

    lax.fori_loop(1, N, send_gated, 0)
    remote(recv3.at[others], recv3.at[others], s3, r3, me_r, me_c).wait_recv()
    update = dot(wo_s[...], recv3[...].reshape(N * SLOT, T))
    out_ref[...] = (x + update[:HEAD]).astype(BF)

    forward.wait_send()
    remote(recv_a.at[0, three], recv_a.at[0, three], sa, ra, me_r, me_c).wait_send()
    remote(columns, columns, sx, rx, me_r, me_c).wait_send()
    remote(send2.at[others], recv2.at[others], s2, r2, me_r, me_c).wait_send()
    remote(recv3.at[others], recv3.at[others], s3, r3, me_r, me_c).wait_send()

    @pl.when(diag)
    def _():
        some = recv_b.at[core, pl.ds(0, N // 2 - 1)]
        remote(some, some, sb, rb, sibling, me_c).wait_send()

    @pl.when(jnp.logical_not(diag))
    def _():
        remote(direct, direct, sb, rb, sibling, me_c).wait_send()


def per_device(
    single, pair, key_mask, chain, single_gain, pair_gain,
    w_query, w_key, w_value, w_gate, w_bias, chain_penalty, w_out,
):
    vmem = pl.BlockSpec(memory_space=pltpu.VMEM)
    hbm = pl.BlockSpec(memory_space=pltpu.HBM)
    out = pl.pallas_call(
        kernel,
        out_shape=pltpu.VMEM((HEAD, T), BF),
        in_specs=[hbm] * 13,
        out_specs=vmem,
        scratch_shapes=[
            pltpu.VMEM((HEAD, T), BF),
            pltpu.VMEM((1, T), jnp.int32),
            pltpu.VMEM((1, T), jnp.int32),
            pltpu.VMEM((1, D), F),
            pltpu.VMEM((1, C), F),
            pltpu.VMEM((N, C), BF),
            pltpu.SMEM((N,), F),
            pltpu.VMEM((T, T, C), BF),
            pltpu.VMEM((N * T, T), F),
            pltpu.VMEM((4, T, 4 * T), F),
            pltpu.VMEM((5, D, D), BF),
            pltpu.VMEM((D, D), BF),
            pltpu.VMEM((2 * D, D), BF),
            pltpu.VMEM((SLOT, D), BF),
            pltpu.VMEM((SLOT, N * SLOT), BF),
            pltpu.VMEM((D, T), F),
            pltpu.VMEM((4, T, T), BF),
            pltpu.VMEM((N, SLOT, T), BF),
            pltpu.VMEM((4, 4 * SLOT, T), BF),
            pltpu.VMEM((SLOT, T), BF),
            pltpu.VMEM((4, 4, SLOT, T), BF),
            pltpu.VMEM((2, N // 2, SLOT, T), BF),
            pltpu.VMEM((N, HEAD // 2 + 1, 2, T), F),
            pltpu.VMEM((N, HEAD // 2 + 1, 2, T), F),
            pltpu.VMEM((SLOT, T), BF),
            pltpu.VMEM((N, SLOT, T), BF),
            pltpu.SemaphoreType.DMA((7,)),
            pltpu.SemaphoreType.DMA((CHUNKS,)),
        ]
        + [pltpu.SemaphoreType.DMA] * 13,
        compiler_params=pltpu.CompilerParams(
            collective_id=0, has_side_effects=True, vmem_limit_bytes=56 << 20
        ),
        name="pair_attention",
    )(
        single.T, key_mask, chain, single_gain, pair_gain, w_bias.T, chain_penalty,
        w_query, w_key, w_value, w_gate, w_out, pair,
    )
    return out.T


def solution(mesh):
    placed = (P("row", "col"), P("row", "col", None), P("row"), P("row")) + (P(),) * 9
    return jax.shard_map(
        per_device, mesh=mesh, in_specs=placed, out_specs=P("row", "col"), check_vma=False
    )
```

```python
import functools

import jax
import jax.numpy as jnp
from jax import lax
from jax.experimental import pallas as pl
from jax.experimental.pallas import tpu as pltpu
from jax.sharding import PartitionSpec as P

BF = jnp.bfloat16
F = jnp.float32
MESH = pl.DeviceIdType.MESH
NN = (((1,), (0,)), ((), ()))
NT = (((1,), (1,)), ((), ()))
N = 16
T = 128
D = 384
HEAD = 24
SLOT = 32
C = 128
CHUNKS = 4
CQ = T // CHUNKS
EARLY = 2
SCALE = 1.0 / 24.0**0.5


def dot(a, b, dims=NN):
    return lax.dot_general(a, b, dims, preferred_element_type=F)


def iota(shape, dim):
    return lax.broadcasted_iota(jnp.int32, shape, dim)


def spread(rows):
    n = rows.shape[1]
    return jnp.concatenate([rows.reshape(N, HEAD, n), jnp.zeros((N, SLOT - HEAD, n), F)], axis=1)


def kernel(
    x_hbm, mask_hbm, chain_hbm, sgain_hbm, pgain_hbm, wb_hbm, pen_hbm,
    wq_hbm, wk_hbm, wv_hbm, wg_hbm, wo_hbm, pair_hbm,
    out_ref,
    x_ref, mask_ref, chain_ref, sgain_ref, pgain_ref, wb_ref, pen_ref,
    pv, bias, bias_t, w_raw, wq_t, wkv_t, wg_s, wo_s, gain_col, kp, qt, vt,
    piece, recv_a, recv_b, send2, recv2, piece3, recv3,
    in_sem, pair_sem, w_sem, sa, ra, sx, rx, sb, rb, sf, rf, s2, r2, s3, r3,
):
    me_r, me_c = lax.axis_index("row"), lax.axis_index("col")
    diag = me_r == me_c
    core, side = lax.rem(me_r, 2), lax.rem(me_c, 2)
    sibling = me_r + 1 - 2 * core
    others, three = pl.ds(0, N - 1), pl.ds(0, 3)
    at_z, at_x = me_c // 4, lax.rem(me_c, 4)

    def pick(first, second):
        return first * (1 - core) + second * core

    at_u, at_v = pick(at_x, at_z), pick(at_z, at_x)

    def along_z(d):
        return lax.rem(at_z + d, 4) * 4 + at_x

    def along_x(d):
        return at_z * 4 + lax.rem(at_x + d, 4)

    def remote(src, dst, send_sem, recv_sem, r, c):
        return pltpu.make_async_remote_copy(
            src_ref=src, dst_ref=dst, send_sem=send_sem, recv_sem=recv_sem,
            device_id=(r, c), device_id_type=MESH,
        )

    def pair_copy(i):
        part = pl.ds(i * CQ, CQ)
        return pltpu.make_async_copy(pair_hbm.at[part], pv.at[part], pair_sem.at[i])

    inputs = [
        pltpu.make_async_copy(src, dst, in_sem.at[i])
        for i, (src, dst) in enumerate(
            (
                (x_hbm, x_ref),
                (mask_hbm, mask_ref.at[0]),
                (chain_hbm, chain_ref.at[0]),
                (sgain_hbm, sgain_ref.at[0]),
                (pgain_hbm, pgain_ref.at[0]),
                (wb_hbm, wb_ref),
                (pen_hbm, pen_ref),
            )
        )
    ]
    for copy in inputs[:3]:
        copy.start()

    barrier = pltpu.get_barrier_semaphore()

    def greet_keys(m, _):
        pl.semaphore_signal(
            barrier,
            inc=1,
            device_id=(me_c, 2 * lax.rem(me_r // 2 + m, N // 2) + core),
            device_id_type=MESH,
        )
        return 0

    lax.fori_loop(1, N // 2, greet_keys, 0)

    @pl.when(jnp.logical_not(diag))
    def _():
        greet_keys(0, 0)

    pl.semaphore_signal(barrier, inc=1, device_id=(sibling, me_c), device_id_type=MESH)
    for d in (1, 2, 3):
        for c in (along_z(d), along_x(d)):
            pl.semaphore_signal(barrier, inc=1, device_id=(me_r, c), device_id_type=MESH)

    for i in range(CHUNKS):
        pair_copy(i).start()

    for copy in inputs[:3]:
        copy.wait()

    x = x_ref[...].astype(F)
    tail_row = iota((SLOT - HEAD, T), 0)
    tail = jnp.where(
        tail_row == 0,
        chain_ref[...].astype(F),
        jnp.where(tail_row == 1, mask_ref[...].astype(F), 0.0),
    )
    mine = jnp.concatenate([x, tail], axis=0).astype(BF)
    piece[...] = mine
    recv_a[at_u, at_v] = mine

    pl.semaphore_wait(barrier, 6 + N // 2 + 1 - diag.astype(jnp.int32))

    def send_keys(m, _):
        r = 2 * lax.rem(me_r // 2 + m, N // 2) + side
        remote(piece, recv_b.at[side, me_c // 2], sb, rb, r, me_r).start()
        return 0

    for d in (1, 2, 3):
        c = pick(along_z(d), along_x(d))
        remote(piece, recv_a.at[at_u, at_v], sa, ra, me_r, c).start()

    lax.fori_loop(1, N // 2, send_keys, 0)

    @pl.when(jnp.logical_not(diag))
    def _():
        send_keys(0, 0)

    @pl.when(diag)
    def _():
        recv_b[side, me_c // 2] = mine

    for copy in inputs[3:]:
        copy.start()
    for i, w in enumerate((wq_hbm, wk_hbm, wv_hbm, wg_hbm, wo_hbm)):
        pltpu.make_async_copy(w, w_raw.at[i], w_sem).start()

    for copy in inputs[3:]:
        copy.wait()

    centre = ((iota((C, C), 0) == iota((C, C), 1)).astype(F) - 1.0 / C).astype(BF)
    pgain = pgain_ref[...]
    wb = wb_ref[...]

    def pair_chunk(i, _):
        pair_copy(i).wait()
        tile = pv[pl.ds(i * CQ, CQ)].reshape(CQ * T, C)
        centered = dot(tile, centre)
        var = jnp.mean(centered * centered, axis=-1, keepdims=True)
        normed = (centered * lax.rsqrt(var + 1e-5) * pgain).astype(BF)
        out = dot(wb, normed, NT)
        for u in range(CQ):
            bias[pl.ds(i * CQ + u, N, stride=T), :] = out[:, u * T : (u + 1) * T]
        return 0

    direct = recv_b.at[core]
    forward = remote(direct, direct, sf, rf, sibling, me_c)
    column, columns = recv_a.at[at_u], recv_a.at[three]

    def pair_step(i, _):
        @pl.when(i == EARLY)
        def _():
            remote(recv_a.at[0, three], recv_a.at[0, three], sa, ra, me_r, me_c).wait_recv()
            for d in (1, 2, 3):
                c = pick(along_x(d), along_z(d))
                remote(column, column, sx, rx, me_r, c).start()

        return pair_chunk(i, 0)

    lax.fori_loop(0, CHUNKS, pair_step, 0)

    @pl.when(diag)
    def _():
        some = recv_b.at[core, pl.ds(0, N // 2 - 1)]
        remote(some, some, sb, rb, sibling, me_c).wait_recv()

    @pl.when(jnp.logical_not(diag))
    def _():
        remote(direct, direct, sb, rb, sibling, me_c).wait_recv()

    forward.start()

    def turn(b, _):
        for j in range(4):
            rows = pl.ds(pl.multiple_of((b * 4 + j) * T, T), T)
            bias_t[b, :, j * T : (j + 1) * T] = bias[rows, :].T
        return 0

    lax.fori_loop(0, 4, turn, 0)

    pltpu.make_async_copy(w_raw, w_raw, w_sem).wait()
    eye_d = (iota((D, D), 0) == iota((D, D), 1)).astype(BF)
    eye_t = (iota((T, T), 0) == iota((T, T), 1)).astype(BF)
    wq_t[...] = dot(eye_d, w_raw[0], NT).astype(BF)
    wkv_t[0:D, :] = dot(eye_d, w_raw[1], NT).astype(BF)
    wkv_t[D : 2 * D, :] = dot(eye_d, w_raw[2], NT).astype(BF)
    own_row = iota((SLOT, D), 0)
    own = ((iota((SLOT, D), 1) == own_row + HEAD * me_c) & (own_row < HEAD)).astype(BF)
    wg_s[...] = dot(own, w_raw[3], NT).astype(BF)
    slot_lane = iota((D, N * SLOT), 1)
    slot_at = lax.rem(slot_lane, SLOT)
    widen = (
        (iota((D, N * SLOT), 0) == (slot_lane // SLOT) * HEAD + slot_at) & (slot_at < HEAD)
    ).astype(BF)
    wo_s[...] = dot(dot(own, w_raw[4], NT).astype(BF), widen).astype(BF)
    for i in range(D // T):
        gain_col[i * T : (i + 1) * T, :] = jnp.broadcast_to(
            sgain_ref[:, i * T : (i + 1) * T], (T, T)
        ).T

    def norm(pieces):
        rows = jnp.concatenate([part.astype(F)[:HEAD] for part in pieces], axis=0)
        centered = rows - jnp.mean(rows, axis=0, keepdims=True)
        var = jnp.mean(centered * centered, axis=0, keepdims=True)
        return (centered * lax.rsqrt(var + 1e-5) * gain_col[...]).astype(BF)

    remote(columns, columns, sx, rx, me_r, me_c).wait_recv()
    normed_q = norm([recv_a[pick(s % 4, s // 4), pick(s // 4, s % 4)] for s in range(N)])
    qt[...] = spread(dot(wq_t[...], normed_q)).astype(BF)
    gate = jax.nn.sigmoid(dot(wg_s[...], normed_q))

    remote(recv_b.at[1 - core], recv_b.at[1 - core], sf, rf, sibling, me_c).wait_recv()
    both = dot(wkv_t[...], norm([recv_b[s % 2, s // 2] for s in range(N)]))
    vt[...] = spread(both[D:]).astype(BF).reshape(4, 4 * SLOT, T)
    keys = dot(eye_t, spread(both[:D]).astype(BF).reshape(N * SLOT, T), NT).astype(BF)
    for b in range(4):
        kp[b] = keys[:, b * T : (b + 1) * T]

    info = recv_b[0, 0].astype(F)
    chain_k = jnp.broadcast_to(info[HEAD : HEAD + 1], (T, T)).T
    mask_k = jnp.broadcast_to(info[HEAD + 1 : HEAD + 2], (T, T)).T
    valid = jnp.concatenate([mask_k] * 4, axis=1) > 0.5
    differ = (chain_k != chain_ref[...].astype(F)).astype(F)
    stat_row = iota((SLOT - HEAD, 4 * T), 0)
    zeros = jnp.zeros((SLOT, T), BF)

    z_hi, z_lo = me_c // 8, lax.rem(me_c // 4, 2)

    def head_half(t, _):
        half = lax.rem(z_hi + 1 + t, 2)
        scores = []
        for p in range(2):
            b = 2 * half + p
            blocks = [
                jnp.concatenate([qt[b * 4 + j] if i == j else zeros for i in range(4)], axis=0)
                for j in range(4)
            ]
            scores.append(dot(kp[b], jnp.concatenate(blocks, axis=1)))
        for p in range(2):
            b = 2 * half + p
            chains = jnp.concatenate([pen_ref[b * 4 + j] * differ for j in range(4)], axis=1)
            score = scores[p] * SCALE + bias_t[b] + chains
            score = jnp.where(valid, score, -1e9)
            top = jnp.max(score, axis=0, keepdims=True)
            expo = jnp.exp(score - top)
            total = jnp.sum(expo, axis=0, keepdims=True)
            weighted = dot(vt[b], expo.astype(BF))
            stats = jnp.where(stat_row == 0, top, jnp.where(stat_row == 1, total, 0.0))
            for j in range(4):
                lanes = slice(j * T, (j + 1) * T)
                sums = weighted[j * SLOT : j * SLOT + HEAD, lanes]
                send2[b * 4 + j, : HEAD // 2] = sums.reshape(HEAD // 2, 2, T)
                send2[b * 4 + j, HEAD // 2] = stats[:2, lanes]

        def send_sums(k, _):
            h = half * 8 + lax.rem(at_x + 1 + k // 2, 4) + 4 * lax.rem(k, 2)

            @pl.when(h != me_c)
            def _():
                remote(send2.at[h], recv2.at[me_c], s2, r2, me_r, h).start()

            @pl.when(h == me_c)
            def _():
                recv2[me_c] = send2[h]

            return 0

        lax.fori_loop(0, 8, send_sums, 0)
        return 0

    lax.fori_loop(0, 2, head_half, 0)

    remote(send2.at[others], recv2.at[others], s2, r2, me_r, me_c).wait_recv()
    stats = recv2[:, HEAD // 2]
    tops = stats[:, 0:1]
    top = jnp.max(tops, axis=0, keepdims=True)
    factor = jnp.exp(tops - top)
    total = jnp.sum(stats[:, 1:2] * factor, axis=0)
    summed = jnp.sum(recv2[:, : HEAD // 2] * factor[:, :, None], axis=0).reshape(HEAD, T)
    gated = summed / total * gate[:HEAD]
    gated = jnp.concatenate([gated, jnp.zeros((SLOT - HEAD, T), F)], axis=0).astype(BF)
    piece3[...] = gated
    recv3[me_c] = gated

    def send_gated(d, _):
        c = lax.rem(me_c + d, N)
        remote(piece3, recv3.at[me_c], s3, r3, me_r, c).start()
        return 0

    for d in range(1, N):
        send_gated(d, 0)
    remote(recv3.at[others], recv3.at[others], s3, r3, me_r, me_c).wait_recv()
    update = dot(wo_s[...], recv3[...].reshape(N * SLOT, T))
    out_ref[...] = (x + update[:HEAD]).astype(BF)

    forward.wait_send()
    remote(recv_a.at[0, three], recv_a.at[0, three], sa, ra, me_r, me_c).wait_send()
    remote(columns, columns, sx, rx, me_r, me_c).wait_send()
    remote(send2.at[others], recv2.at[others], s2, r2, me_r, me_c).wait_send()
    remote(recv3.at[others], recv3.at[others], s3, r3, me_r, me_c).wait_send()

    @pl.when(diag)
    def _():
        some = recv_b.at[core, pl.ds(0, N // 2 - 1)]
        remote(some, some, sb, rb, sibling, me_c).wait_send()

    @pl.when(jnp.logical_not(diag))
    def _():
        remote(direct, direct, sb, rb, sibling, me_c).wait_send()


def per_device(
    single, pair, key_mask, chain, single_gain, pair_gain,
    w_query, w_key, w_value, w_gate, w_bias, chain_penalty, w_out,
):
    vmem = pl.BlockSpec(memory_space=pltpu.VMEM)
    hbm = pl.BlockSpec(memory_space=pltpu.HBM)
    out = pl.pallas_call(
        kernel,
        out_shape=pltpu.VMEM((HEAD, T), BF),
        in_specs=[hbm] * 13,
        out_specs=vmem,
        scratch_shapes=[
            pltpu.VMEM((HEAD, T), BF),
            pltpu.VMEM((1, T), jnp.int32),
            pltpu.VMEM((1, T), jnp.int32),
            pltpu.VMEM((1, D), F),
            pltpu.VMEM((1, C), F),
            pltpu.VMEM((N, C), BF),
            pltpu.SMEM((N,), F),
            pltpu.VMEM((T, T, C), BF),
            pltpu.VMEM((N * T, T), F),
            pltpu.VMEM((4, T, 4 * T), F),
            pltpu.VMEM((5, D, D), BF),
            pltpu.VMEM((D, D), BF),
            pltpu.VMEM((2 * D, D), BF),
            pltpu.VMEM((SLOT, D), BF),
            pltpu.VMEM((SLOT, N * SLOT), BF),
            pltpu.VMEM((D, T), F),
            pltpu.VMEM((4, T, T), BF),
            pltpu.VMEM((N, SLOT, T), BF),
            pltpu.VMEM((4, 4 * SLOT, T), BF),
            pltpu.VMEM((SLOT, T), BF),
            pltpu.VMEM((4, 4, SLOT, T), BF),
            pltpu.VMEM((2, N // 2, SLOT, T), BF),
            pltpu.VMEM((N, HEAD // 2 + 1, 2, T), F),
            pltpu.VMEM((N, HEAD // 2 + 1, 2, T), F),
            pltpu.VMEM((SLOT, T), BF),
            pltpu.VMEM((N, SLOT, T), BF),
            pltpu.SemaphoreType.DMA((7,)),
            pltpu.SemaphoreType.DMA((CHUNKS,)),
        ]
        + [pltpu.SemaphoreType.DMA] * 13,
        compiler_params=pltpu.CompilerParams(
            collective_id=0, has_side_effects=True, vmem_limit_bytes=56 << 20
        ),
        name="pair_attention",
    )(
        single.T, key_mask, chain, single_gain, pair_gain, w_bias.T, chain_penalty,
        w_query, w_key, w_value, w_gate, w_out, pair,
    )
    return out.T


def solution(mesh):
    placed = (P("row", "col"), P("row", "col", None), P("row"), P("row")) + (P(),) * 9
    return jax.shard_map(
        per_device, mesh=mesh, in_specs=placed, out_specs=P("row", "col"), check_vma=False
    )
```

```python
import functools

import jax
import jax.numpy as jnp
from jax import lax
from jax.experimental import pallas as pl
from jax.experimental.pallas import tpu as pltpu
from jax.sharding import PartitionSpec as P

BF = jnp.bfloat16
F = jnp.float32
MESH = pl.DeviceIdType.MESH
NN = (((1,), (0,)), ((), ()))
NT = (((1,), (1,)), ((), ()))
N = 16
T = 128
D = 384
HEAD = 24
SLOT = 32
C = 128
CHUNKS = 4
CQ = T // CHUNKS
EARLY = 2
SCALE = 1.0 / 24.0**0.5


def dot(a, b, dims=NN):
    return lax.dot_general(a, b, dims, preferred_element_type=F)


def iota(shape, dim):
    return lax.broadcasted_iota(jnp.int32, shape, dim)


def spread(rows):
    n = rows.shape[1]
    return jnp.concatenate([rows.reshape(N, HEAD, n), jnp.zeros((N, SLOT - HEAD, n), F)], axis=1)


def kernel(
    x_hbm, mask_hbm, chain_hbm, sgain_hbm, pgain_hbm, wb_hbm, pen_hbm,
    wq_hbm, wk_hbm, wv_hbm, wg_hbm, wo_hbm, pair_hbm,
    out_ref,
    x_ref, mask_ref, chain_ref, sgain_ref, pgain_ref, wb_ref, pen_ref,
    pv, bias, bias_t, w_raw, wq_t, wkv_t, wg_s, wo_s, gain_col, kp, qt, vt,
    piece, recv_a, recv_b, send2, recv2, piece3, recv3,
    in_sem, pair_sem, w_sem, sa, ra, sx, rx, sb, rb, sf, rf, s2, r2, s3, r3,
):
    me_r, me_c = lax.axis_index("row"), lax.axis_index("col")
    diag = me_r == me_c
    core, side = lax.rem(me_r, 2), lax.rem(me_c, 2)
    sibling = me_r + 1 - 2 * core
    others, three = pl.ds(0, N - 1), pl.ds(0, 3)
    at_z, at_x = me_c // 4, lax.rem(me_c, 4)

    def pick(first, second):
        return first * (1 - core) + second * core

    at_u, at_v = pick(at_x, at_z), pick(at_z, at_x)

    def along_z(d):
        return lax.rem(at_z + d, 4) * 4 + at_x

    def along_x(d):
        return at_z * 4 + lax.rem(at_x + d, 4)

    def remote(src, dst, send_sem, recv_sem, r, c):
        return pltpu.make_async_remote_copy(
            src_ref=src, dst_ref=dst, send_sem=send_sem, recv_sem=recv_sem,
            device_id=(r, c), device_id_type=MESH,
        )

    def pair_copy(i):
        part = pl.ds(i * CQ, CQ)
        return pltpu.make_async_copy(pair_hbm.at[part], pv.at[part], pair_sem.at[i])

    inputs = [
        pltpu.make_async_copy(src, dst, in_sem.at[i])
        for i, (src, dst) in enumerate(
            (
                (x_hbm, x_ref),
                (mask_hbm, mask_ref.at[0]),
                (chain_hbm, chain_ref.at[0]),
                (sgain_hbm, sgain_ref.at[0]),
                (pgain_hbm, pgain_ref.at[0]),
                (wb_hbm, wb_ref),
                (pen_hbm, pen_ref),
            )
        )
    ]

    barrier = pltpu.get_barrier_semaphore()

    def greet_keys(m, _):
        pl.semaphore_signal(
            barrier,
            inc=1,
            device_id=(me_c, 2 * lax.rem(me_r // 2 + m, N // 2) + core),
            device_id_type=MESH,
        )
        return 0

    lax.fori_loop(1, N // 2, greet_keys, 0)

    @pl.when(jnp.logical_not(diag))
    def _():
        greet_keys(0, 0)

    pl.semaphore_signal(barrier, inc=1, device_id=(sibling, me_c), device_id_type=MESH)
    for d in (1, 2, 3):
        for c in (along_z(d), along_x(d)):
            pl.semaphore_signal(barrier, inc=1, device_id=(me_r, c), device_id_type=MESH)

    for copy in inputs[:3]:
        copy.start()

    for i in range(CHUNKS):
        pair_copy(i).start()

    for copy in inputs[:3]:
        copy.wait()

    x = x_ref[...].astype(F)
    tail_row = iota((SLOT - HEAD, T), 0)
    tail = jnp.where(
        tail_row == 0,
        chain_ref[...].astype(F),
        jnp.where(tail_row == 1, mask_ref[...].astype(F), 0.0),
    )
    mine = jnp.concatenate([x, tail], axis=0).astype(BF)
    piece[...] = mine
    recv_a[at_u, at_v] = mine

    pl.semaphore_wait(barrier, 6 + N // 2 + 1 - diag.astype(jnp.int32))

    def send_keys(m, _):
        r = 2 * lax.rem(me_r // 2 + m, N // 2) + side
        remote(piece, recv_b.at[side, me_c // 2], sb, rb, r, me_r).start()
        return 0

    for d in (1, 2, 3):
        c = pick(along_z(d), along_x(d))
        remote(piece, recv_a.at[at_u, at_v], sa, ra, me_r, c).start()

    lax.fori_loop(1, N // 2, send_keys, 0)

    @pl.when(jnp.logical_not(diag))
    def _():
        send_keys(0, 0)

    @pl.when(diag)
    def _():
        recv_b[side, me_c // 2] = mine

    for copy in inputs[3:]:
        copy.start()
    for i, w in enumerate((wq_hbm, wk_hbm, wv_hbm, wg_hbm, wo_hbm)):
        pltpu.make_async_copy(w, w_raw.at[i], w_sem).start()

    for copy in inputs[3:]:
        copy.wait()

    centre = ((iota((C, C), 0) == iota((C, C), 1)).astype(F) - 1.0 / C).astype(BF)
    pgain = pgain_ref[...]
    wb = wb_ref[...]

    def pair_chunk(i, _):
        pair_copy(i).wait()
        tile = pv[pl.ds(i * CQ, CQ)].reshape(CQ * T, C)
        centered = dot(tile, centre)
        var = jnp.mean(centered * centered, axis=-1, keepdims=True)
        normed = (centered * lax.rsqrt(var + 1e-5) * pgain).astype(BF)
        out = dot(wb, normed, NT)
        for u in range(CQ):
            bias[pl.ds(i * CQ + u, N, stride=T), :] = out[:, u * T : (u + 1) * T]
        return 0

    direct = recv_b.at[core]
    forward = remote(direct, direct, sf, rf, sibling, me_c)
    column, columns = recv_a.at[at_u], recv_a.at[three]

    def pair_step(i, _):
        @pl.when(i == EARLY)
        def _():
            remote(recv_a.at[0, three], recv_a.at[0, three], sa, ra, me_r, me_c).wait_recv()
            for d in (1, 2, 3):
                c = pick(along_x(d), along_z(d))
                remote(column, column, sx, rx, me_r, c).start()

        return pair_chunk(i, 0)

    lax.fori_loop(0, CHUNKS, pair_step, 0)

    @pl.when(diag)
    def _():
        some = recv_b.at[core, pl.ds(0, N // 2 - 1)]
        remote(some, some, sb, rb, sibling, me_c).wait_recv()

    @pl.when(jnp.logical_not(diag))
    def _():
        remote(direct, direct, sb, rb, sibling, me_c).wait_recv()

    forward.start()

    def turn(b, _):
        for j in range(4):
            rows = pl.ds(pl.multiple_of((b * 4 + j) * T, T), T)
            bias_t[b, :, j * T : (j + 1) * T] = bias[rows, :].T
        return 0

    lax.fori_loop(0, 4, turn, 0)

    pltpu.make_async_copy(w_raw, w_raw, w_sem).wait()
    eye_d = (iota((D, D), 0) == iota((D, D), 1)).astype(BF)
    eye_t = (iota((T, T), 0) == iota((T, T), 1)).astype(BF)
    wq_t[...] = dot(eye_d, w_raw[0], NT).astype(BF)
    wkv_t[0:D, :] = dot(eye_d, w_raw[1], NT).astype(BF)
    wkv_t[D : 2 * D, :] = dot(eye_d, w_raw[2], NT).astype(BF)
    own_row = iota((SLOT, D), 0)
    own = ((iota((SLOT, D), 1) == own_row + HEAD * me_c) & (own_row < HEAD)).astype(BF)
    wg_s[...] = dot(own, w_raw[3], NT).astype(BF)
    slot_lane = iota((D, N * SLOT), 1)
    slot_at = lax.rem(slot_lane, SLOT)
    widen = (
        (iota((D, N * SLOT), 0) == (slot_lane // SLOT) * HEAD + slot_at) & (slot_at < HEAD)
    ).astype(BF)
    wo_s[...] = dot(dot(own, w_raw[4], NT).astype(BF), widen).astype(BF)
    for i in range(D // T):
        gain_col[i * T : (i + 1) * T, :] = jnp.broadcast_to(
            sgain_ref[:, i * T : (i + 1) * T], (T, T)
        ).T

    def norm(pieces):
        rows = jnp.concatenate([part.astype(F)[:HEAD] for part in pieces], axis=0)
        centered = rows - jnp.mean(rows, axis=0, keepdims=True)
        var = jnp.mean(centered * centered, axis=0, keepdims=True)
        return (centered * lax.rsqrt(var + 1e-5) * gain_col[...]).astype(BF)

    remote(columns, columns, sx, rx, me_r, me_c).wait_recv()
    normed_q = norm([recv_a[pick(s % 4, s // 4), pick(s // 4, s % 4)] for s in range(N)])
    qt[...] = spread(dot(wq_t[...], normed_q)).astype(BF)
    gate = jax.nn.sigmoid(dot(wg_s[...], normed_q))

    remote(recv_b.at[1 - core], recv_b.at[1 - core], sf, rf, sibling, me_c).wait_recv()
    both = dot(wkv_t[...], norm([recv_b[s % 2, s // 2] for s in range(N)]))
    vt[...] = spread(both[D:]).astype(BF).reshape(4, 4 * SLOT, T)
    keys = dot(eye_t, spread(both[:D]).astype(BF).reshape(N * SLOT, T), NT).astype(BF)
    for b in range(4):
        kp[b] = keys[:, b * T : (b + 1) * T]

    info = recv_b[0, 0].astype(F)
    chain_k = jnp.broadcast_to(info[HEAD : HEAD + 1], (T, T)).T
    mask_k = jnp.broadcast_to(info[HEAD + 1 : HEAD + 2], (T, T)).T
    valid = jnp.concatenate([mask_k] * 4, axis=1) > 0.5
    differ = (chain_k != chain_ref[...].astype(F)).astype(F)
    stat_row = iota((SLOT - HEAD, 4 * T), 0)
    zeros = jnp.zeros((SLOT, T), BF)

    z_hi, z_lo = me_c // 8, lax.rem(me_c // 4, 2)

    def head_half(t, _):
        half = lax.rem(z_hi + 1 + t, 2)
        scores = []
        for p in range(2):
            b = 2 * half + p
            blocks = [
                jnp.concatenate([qt[b * 4 + j] if i == j else zeros for i in range(4)], axis=0)
                for j in range(4)
            ]
            scores.append(dot(kp[b], jnp.concatenate(blocks, axis=1)))
        for p in range(2):
            b = 2 * half + p
            chains = jnp.concatenate([pen_ref[b * 4 + j] * differ for j in range(4)], axis=1)
            score = scores[p] * SCALE + bias_t[b] + chains
            score = jnp.where(valid, score, -1e9)
            top = jnp.max(score, axis=0, keepdims=True)
            expo = jnp.exp(score - top)
            total = jnp.sum(expo, axis=0, keepdims=True)
            weighted = dot(vt[b], expo.astype(BF))
            stats = jnp.where(stat_row == 0, top, jnp.where(stat_row == 1, total, 0.0))
            for j in range(4):
                lanes = slice(j * T, (j + 1) * T)
                sums = weighted[j * SLOT : j * SLOT + HEAD, lanes]
                send2[b * 4 + j, : HEAD // 2] = sums.reshape(HEAD // 2, 2, T)
                send2[b * 4 + j, HEAD // 2] = stats[:2, lanes]

        def send_sums(k, _):
            h = half * 8 + lax.rem(at_x + 1 + k // 2, 4) + 4 * lax.rem(k, 2)

            @pl.when(h != me_c)
            def _():
                remote(send2.at[h], recv2.at[me_c], s2, r2, me_r, h).start()

            @pl.when(h == me_c)
            def _():
                recv2[me_c] = send2[h]

            return 0

        lax.fori_loop(0, 8, send_sums, 0)
        return 0

    lax.fori_loop(0, 2, head_half, 0)

    remote(send2.at[others], recv2.at[others], s2, r2, me_r, me_c).wait_recv()
    stats = recv2[:, HEAD // 2]
    tops = stats[:, 0:1]
    top = jnp.max(tops, axis=0, keepdims=True)
    factor = jnp.exp(tops - top)
    total = jnp.sum(stats[:, 1:2] * factor, axis=0)
    summed = jnp.sum(recv2[:, : HEAD // 2] * factor[:, :, None], axis=0).reshape(HEAD, T)
    gated = summed / total * gate[:HEAD]
    gated = jnp.concatenate([gated, jnp.zeros((SLOT - HEAD, T), F)], axis=0).astype(BF)
    piece3[...] = gated
    recv3[me_c] = gated

    def send_gated(d, _):
        c = lax.rem(me_c + d, N)
        remote(piece3, recv3.at[me_c], s3, r3, me_r, c).start()
        return 0

    for d in range(1, N):
        send_gated(d, 0)
    forward.wait_send()
    remote(recv_a.at[0, three], recv_a.at[0, three], sa, ra, me_r, me_c).wait_send()
    remote(columns, columns, sx, rx, me_r, me_c).wait_send()
    remote(send2.at[others], recv2.at[others], s2, r2, me_r, me_c).wait_send()

    @pl.when(diag)
    def _():
        some = recv_b.at[core, pl.ds(0, N // 2 - 1)]
        remote(some, some, sb, rb, sibling, me_c).wait_send()

    @pl.when(jnp.logical_not(diag))
    def _():
        remote(direct, direct, sb, rb, sibling, me_c).wait_send()

    remote(recv3.at[others], recv3.at[others], s3, r3, me_r, me_c).wait_recv()
    update = dot(wo_s[...], recv3[...].reshape(N * SLOT, T))
    out_ref[...] = (x + update[:HEAD]).astype(BF)

    remote(recv3.at[others], recv3.at[others], s3, r3, me_r, me_c).wait_send()


def per_device(
    single, pair, key_mask, chain, single_gain, pair_gain,
    w_query, w_key, w_value, w_gate, w_bias, chain_penalty, w_out,
):
    vmem = pl.BlockSpec(memory_space=pltpu.VMEM)
    hbm = pl.BlockSpec(memory_space=pltpu.HBM)
    out = pl.pallas_call(
        kernel,
        out_shape=pltpu.VMEM((HEAD, T), BF),
        in_specs=[hbm] * 13,
        out_specs=vmem,
        scratch_shapes=[
            pltpu.VMEM((HEAD, T), BF),
            pltpu.VMEM((1, T), jnp.int32),
            pltpu.VMEM((1, T), jnp.int32),
            pltpu.VMEM((1, D), F),
            pltpu.VMEM((1, C), F),
            pltpu.VMEM((N, C), BF),
            pltpu.SMEM((N,), F),
            pltpu.VMEM((T, T, C), BF),
            pltpu.VMEM((N * T, T), F),
            pltpu.VMEM((4, T, 4 * T), F),
            pltpu.VMEM((5, D, D), BF),
            pltpu.VMEM((D, D), BF),
            pltpu.VMEM((2 * D, D), BF),
            pltpu.VMEM((SLOT, D), BF),
            pltpu.VMEM((SLOT, N * SLOT), BF),
            pltpu.VMEM((D, T), F),
            pltpu.VMEM((4, T, T), BF),
            pltpu.VMEM((N, SLOT, T), BF),
            pltpu.VMEM((4, 4 * SLOT, T), BF),
            pltpu.VMEM((SLOT, T), BF),
            pltpu.VMEM((4, 4, SLOT, T), BF),
            pltpu.VMEM((2, N // 2, SLOT, T), BF),
            pltpu.VMEM((N, HEAD // 2 + 1, 2, T), F),
            pltpu.VMEM((N, HEAD // 2 + 1, 2, T), F),
            pltpu.VMEM((SLOT, T), BF),
            pltpu.VMEM((N, SLOT, T), BF),
            pltpu.SemaphoreType.DMA((7,)),
            pltpu.SemaphoreType.DMA((CHUNKS,)),
        ]
        + [pltpu.SemaphoreType.DMA] * 13,
        compiler_params=pltpu.CompilerParams(
            collective_id=0, has_side_effects=True, vmem_limit_bytes=56 << 20
        ),
        name="pair_attention",
    )(
        single.T, key_mask, chain, single_gain, pair_gain, w_bias.T, chain_penalty,
        w_query, w_key, w_value, w_gate, w_out, pair,
    )
    return out.T


def solution(mesh):
    placed = (P("row", "col"), P("row", "col", None), P("row"), P("row")) + (P(),) * 9
    return jax.shard_map(
        per_device, mesh=mesh, in_specs=placed, out_specs=P("row", "col"), check_vma=False
    )
```

```python
import functools

import jax
import jax.numpy as jnp
from jax import lax
from jax.experimental import pallas as pl
from jax.experimental.pallas import tpu as pltpu
from jax.sharding import PartitionSpec as P

BF = jnp.bfloat16
F = jnp.float32
MESH = pl.DeviceIdType.MESH
NN = (((1,), (0,)), ((), ()))
NT = (((1,), (1,)), ((), ()))
N = 16
T = 128
D = 384
HEAD = 24
SLOT = 32
C = 128
CHUNKS = 4
CQ = T // CHUNKS
AHEAD = 2
SCALE = 1.0 / 24.0**0.5


def dot(a, b, dims=NN):
    return lax.dot_general(a, b, dims, preferred_element_type=F)


def iota(shape, dim):
    return lax.broadcasted_iota(jnp.int32, shape, dim)


def spread(rows):
    n = rows.shape[1]
    return jnp.concatenate([rows.reshape(N, HEAD, n), jnp.zeros((N, SLOT - HEAD, n), F)], axis=1)


def kernel(
    x_hbm, mask_hbm, chain_hbm, sgain_hbm, pgain_hbm, wb_hbm, pen_hbm,
    wq_hbm, wk_hbm, wv_hbm, wg_hbm, wo_hbm, pair_hbm,
    out_ref,
    x_ref, mask_ref, chain_ref, sgain_ref, pgain_ref, wb_ref, pen_ref,
    pv, bias, bias_t, w_raw, wq_t, wkv_t, wg_s, wo_s, gain_col, kp, qt, vt,
    piece, recv_a, recv_b, send2, recv2, piece3, recv3,
    in_sem, pair_sem, w_sem, sa, ra, sx, rx, sb, rb, sf, rf, s2, r2, s3, r3,
):
    me_r, me_c = lax.axis_index("row"), lax.axis_index("col")
    diag = me_r == me_c
    core, side = lax.rem(me_r, 2), lax.rem(me_c, 2)
    sibling = me_r + 1 - 2 * core
    others, three = pl.ds(0, N - 1), pl.ds(0, 3)
    at_z, at_x = me_c // 4, lax.rem(me_c, 4)

    def pick(first, second):
        return first * (1 - core) + second * core

    at_u, at_v = pick(at_x, at_z), pick(at_z, at_x)

    def along_z(d):
        return lax.rem(at_z + d, 4) * 4 + at_x

    def along_x(d):
        return at_z * 4 + lax.rem(at_x + d, 4)

    def remote(src, dst, send_sem, recv_sem, r, c):
        return pltpu.make_async_remote_copy(
            src_ref=src, dst_ref=dst, send_sem=send_sem, recv_sem=recv_sem,
            device_id=(r, c), device_id_type=MESH,
        )

    def pair_copy(i):
        part = pl.ds(i * CQ, CQ)
        return pltpu.make_async_copy(pair_hbm.at[part], pv.at[part], pair_sem.at[i])

    inputs = [
        pltpu.make_async_copy(src, dst, in_sem.at[i])
        for i, (src, dst) in enumerate(
            (
                (x_hbm, x_ref),
                (mask_hbm, mask_ref.at[0]),
                (chain_hbm, chain_ref.at[0]),
                (sgain_hbm, sgain_ref.at[0]),
                (pgain_hbm, pgain_ref.at[0]),
                (wb_hbm, wb_ref),
                (pen_hbm, pen_ref),
            )
        )
    ]

    barrier = pltpu.get_barrier_semaphore()

    def greet_keys(m, _):
        pl.semaphore_signal(
            barrier,
            inc=1,
            device_id=(me_c, 2 * lax.rem(me_r // 2 + m, N // 2) + core),
            device_id_type=MESH,
        )
        return 0

    lax.fori_loop(1, N // 2, greet_keys, 0)

    @pl.when(jnp.logical_not(diag))
    def _():
        greet_keys(0, 0)

    pl.semaphore_signal(barrier, inc=1, device_id=(sibling, me_c), device_id_type=MESH)
    for d in (1, 2, 3):
        for c in (along_z(d), along_x(d)):
            pl.semaphore_signal(barrier, inc=1, device_id=(me_r, c), device_id_type=MESH)

    for copy in inputs[:3]:
        copy.start()

    for copy in inputs[3:]:
        copy.start()
    for i in range(CHUNKS):
        pair_copy(i).start()

    for copy in inputs[:3]:
        copy.wait()

    x = x_ref[...].astype(F)
    tail_row = iota((SLOT - HEAD, T), 0)
    tail = jnp.where(
        tail_row == 0,
        chain_ref[...].astype(F),
        jnp.where(tail_row == 1, mask_ref[...].astype(F), 0.0),
    )
    mine = jnp.concatenate([x, tail], axis=0).astype(BF)
    piece[...] = mine
    recv_a[at_u, at_v] = mine

    for copy in inputs[3:]:
        copy.wait()

    centre = ((iota((C, C), 0) == iota((C, C), 1)).astype(F) - 1.0 / C).astype(BF)
    pgain = pgain_ref[...]
    wb = wb_ref[...]

    def pair_chunk(i, _):
        pair_copy(i).wait()
        tile = pv[pl.ds(i * CQ, CQ)].reshape(CQ * T, C)
        centered = dot(tile, centre)
        var = jnp.mean(centered * centered, axis=-1, keepdims=True)
        normed = (centered * lax.rsqrt(var + 1e-5) * pgain).astype(BF)
        out = dot(wb, normed, NT)
        for u in range(CQ):
            bias[pl.ds(i * CQ + u, N, stride=T), :] = out[:, u * T : (u + 1) * T]
        return 0

    second = me_r // 8
    begun = AHEAD * (1 - second)
    lax.fori_loop(0, begun, pair_chunk, 0)
    pl.semaphore_wait(barrier, 6 + N // 2 + 1 - diag.astype(jnp.int32))

    def send_keys(m, _):
        r = 2 * lax.rem(me_r // 2 + m, N // 2) + side
        remote(piece, recv_b.at[side, me_c // 2], sb, rb, r, me_r).start()
        return 0

    for d in (1, 2, 3):
        c = pick(along_z(d), along_x(d))
        remote(piece, recv_a.at[at_u, at_v], sa, ra, me_r, c).start()

    lax.fori_loop(1, N // 2, send_keys, 0)

    @pl.when(jnp.logical_not(diag))
    def _():
        send_keys(0, 0)

    @pl.when(diag)
    def _():
        recv_b[side, me_c // 2] = mine

    for i, w in enumerate((wq_hbm, wk_hbm, wv_hbm, wg_hbm, wo_hbm)):
        pltpu.make_async_copy(w, w_raw.at[i], w_sem).start()

    direct = recv_b.at[core]
    forward = remote(direct, direct, sf, rf, sibling, me_c)
    column, columns = recv_a.at[at_u], recv_a.at[three]

    def pair_step(i, _):
        @pl.when(i == 3 - second)
        def _():
            remote(recv_a.at[0, three], recv_a.at[0, three], sa, ra, me_r, me_c).wait_recv()
            for d in (1, 2, 3):
                c = pick(along_x(d), along_z(d))
                remote(column, column, sx, rx, me_r, c).start()

        return pair_chunk(i, 0)

    lax.fori_loop(begun, CHUNKS, pair_step, 0)

    @pl.when(diag)
    def _():
        some = recv_b.at[core, pl.ds(0, N // 2 - 1)]
        remote(some, some, sb, rb, sibling, me_c).wait_recv()

    @pl.when(jnp.logical_not(diag))
    def _():
        remote(direct, direct, sb, rb, sibling, me_c).wait_recv()

    forward.start()

    def turn(b, _):
        for j in range(4):
            rows = pl.ds(pl.multiple_of((b * 4 + j) * T, T), T)
            bias_t[b, :, j * T : (j + 1) * T] = bias[rows, :].T
        return 0

    lax.fori_loop(0, 4, turn, 0)

    pltpu.make_async_copy(w_raw, w_raw, w_sem).wait()
    eye_d = (iota((D, D), 0) == iota((D, D), 1)).astype(BF)
    eye_t = (iota((T, T), 0) == iota((T, T), 1)).astype(BF)
    wq_t[...] = dot(eye_d, w_raw[0], NT).astype(BF)
    wkv_t[0:D, :] = dot(eye_d, w_raw[1], NT).astype(BF)
    wkv_t[D : 2 * D, :] = dot(eye_d, w_raw[2], NT).astype(BF)
    own_row = iota((SLOT, D), 0)
    own = ((iota((SLOT, D), 1) == own_row + HEAD * me_c) & (own_row < HEAD)).astype(BF)
    wg_s[...] = dot(own, w_raw[3], NT).astype(BF)
    slot_lane = iota((D, N * SLOT), 1)
    slot_at = lax.rem(slot_lane, SLOT)
    widen = (
        (iota((D, N * SLOT), 0) == (slot_lane // SLOT) * HEAD + slot_at) & (slot_at < HEAD)
    ).astype(BF)
    wo_s[...] = dot(dot(own, w_raw[4], NT).astype(BF), widen).astype(BF)
    for i in range(D // T):
        gain_col[i * T : (i + 1) * T, :] = jnp.broadcast_to(
            sgain_ref[:, i * T : (i + 1) * T], (T, T)
        ).T

    def norm(pieces):
        rows = jnp.concatenate([part.astype(F)[:HEAD] for part in pieces], axis=0)
        centered = rows - jnp.mean(rows, axis=0, keepdims=True)
        var = jnp.mean(centered * centered, axis=0, keepdims=True)
        return (centered * lax.rsqrt(var + 1e-5) * gain_col[...]).astype(BF)

    remote(columns, columns, sx, rx, me_r, me_c).wait_recv()
    normed_q = norm([recv_a[pick(s % 4, s // 4), pick(s // 4, s % 4)] for s in range(N)])
    qt[...] = spread(dot(wq_t[...], normed_q)).astype(BF)
    gate = jax.nn.sigmoid(dot(wg_s[...], normed_q))

    remote(recv_b.at[1 - core], recv_b.at[1 - core], sf, rf, sibling, me_c).wait_recv()
    both = dot(wkv_t[...], norm([recv_b[s % 2, s // 2] for s in range(N)]))
    vt[...] = spread(both[D:]).astype(BF).reshape(4, 4 * SLOT, T)
    keys = dot(eye_t, spread(both[:D]).astype(BF).reshape(N * SLOT, T), NT).astype(BF)
    for b in range(4):
        kp[b] = keys[:, b * T : (b + 1) * T]

    info = recv_b[0, 0].astype(F)
    chain_k = jnp.broadcast_to(info[HEAD : HEAD + 1], (T, T)).T
    mask_k = jnp.broadcast_to(info[HEAD + 1 : HEAD + 2], (T, T)).T
    valid = jnp.concatenate([mask_k] * 4, axis=1) > 0.5
    differ = (chain_k != chain_ref[...].astype(F)).astype(F)
    stat_row = iota((SLOT - HEAD, 4 * T), 0)
    zeros = jnp.zeros((SLOT, T), BF)

    z_hi, z_lo = me_c // 8, lax.rem(me_c // 4, 2)

    def head_half(t, _):
        half = lax.rem(z_hi + 1 + t, 2)
        scores = []
        for p in range(2):
            b = 2 * half + p
            blocks = [
                jnp.concatenate([qt[b * 4 + j] if i == j else zeros for i in range(4)], axis=0)
                for j in range(4)
            ]
            scores.append(dot(kp[b], jnp.concatenate(blocks, axis=1)))
        for p in range(2):
            b = 2 * half + p
            chains = jnp.concatenate([pen_ref[b * 4 + j] * differ for j in range(4)], axis=1)
            score = scores[p] * SCALE + bias_t[b] + chains
            score = jnp.where(valid, score, -1e9)
            top = jnp.max(score, axis=0, keepdims=True)
            expo = jnp.exp(score - top)
            total = jnp.sum(expo, axis=0, keepdims=True)
            weighted = dot(vt[b], expo.astype(BF))
            stats = jnp.where(stat_row == 0, top, jnp.where(stat_row == 1, total, 0.0))
            for j in range(4):
                lanes = slice(j * T, (j + 1) * T)
                sums = weighted[j * SLOT : j * SLOT + HEAD, lanes]
                send2[b * 4 + j, : HEAD // 2] = sums.reshape(HEAD // 2, 2, T)
                send2[b * 4 + j, HEAD // 2] = stats[:2, lanes]

        def send_sums(k, _):
            h = half * 8 + lax.rem(at_x + 1 + k // 2, 4) + 4 * lax.rem(k, 2)

            @pl.when(h != me_c)
            def _():
                remote(send2.at[h], recv2.at[me_c], s2, r2, me_r, h).start()

            @pl.when(h == me_c)
            def _():
                recv2[me_c] = send2[h]

            return 0

        lax.fori_loop(0, 8, send_sums, 0)
        return 0

    lax.fori_loop(0, 2, head_half, 0)

    remote(send2.at[others], recv2.at[others], s2, r2, me_r, me_c).wait_recv()
    stats = recv2[:, HEAD // 2]
    tops = stats[:, 0:1]
    top = jnp.max(tops, axis=0, keepdims=True)
    factor = jnp.exp(tops - top)
    total = jnp.sum(stats[:, 1:2] * factor, axis=0)
    summed = jnp.sum(recv2[:, : HEAD // 2] * factor[:, :, None], axis=0).reshape(HEAD, T)
    gated = summed / total * gate[:HEAD]
    gated = jnp.concatenate([gated, jnp.zeros((SLOT - HEAD, T), F)], axis=0).astype(BF)
    piece3[...] = gated
    recv3[me_c] = gated

    def send_gated(d, _):
        c = lax.rem(me_c + d, N)
        remote(piece3, recv3.at[me_c], s3, r3, me_r, c).start()
        return 0

    for d in range(1, N):
        send_gated(d, 0)
    forward.wait_send()
    remote(recv_a.at[0, three], recv_a.at[0, three], sa, ra, me_r, me_c).wait_send()
    remote(columns, columns, sx, rx, me_r, me_c).wait_send()
    remote(send2.at[others], recv2.at[others], s2, r2, me_r, me_c).wait_send()

    @pl.when(diag)
    def _():
        some = recv_b.at[core, pl.ds(0, N // 2 - 1)]
        remote(some, some, sb, rb, sibling, me_c).wait_send()

    @pl.when(jnp.logical_not(diag))
    def _():
        remote(direct, direct, sb, rb, sibling, me_c).wait_send()

    remote(recv3.at[others], recv3.at[others], s3, r3, me_r, me_c).wait_recv()
    update = dot(wo_s[...], recv3[...].reshape(N * SLOT, T))
    out_ref[...] = (x + update[:HEAD]).astype(BF)

    remote(recv3.at[others], recv3.at[others], s3, r3, me_r, me_c).wait_send()


def per_device(
    single, pair, key_mask, chain, single_gain, pair_gain,
    w_query, w_key, w_value, w_gate, w_bias, chain_penalty, w_out,
):
    vmem = pl.BlockSpec(memory_space=pltpu.VMEM)
    hbm = pl.BlockSpec(memory_space=pltpu.HBM)
    out = pl.pallas_call(
        kernel,
        out_shape=pltpu.VMEM((HEAD, T), BF),
        in_specs=[hbm] * 13,
        out_specs=vmem,
        scratch_shapes=[
            pltpu.VMEM((HEAD, T), BF),
            pltpu.VMEM((1, T), jnp.int32),
            pltpu.VMEM((1, T), jnp.int32),
            pltpu.VMEM((1, D), F),
            pltpu.VMEM((1, C), F),
            pltpu.VMEM((N, C), BF),
            pltpu.SMEM((N,), F),
            pltpu.VMEM((T, T, C), BF),
            pltpu.VMEM((N * T, T), F),
            pltpu.VMEM((4, T, 4 * T), F),
            pltpu.VMEM((5, D, D), BF),
            pltpu.VMEM((D, D), BF),
            pltpu.VMEM((2 * D, D), BF),
            pltpu.VMEM((SLOT, D), BF),
            pltpu.VMEM((SLOT, N * SLOT), BF),
            pltpu.VMEM((D, T), F),
            pltpu.VMEM((4, T, T), BF),
            pltpu.VMEM((N, SLOT, T), BF),
            pltpu.VMEM((4, 4 * SLOT, T), BF),
            pltpu.VMEM((SLOT, T), BF),
            pltpu.VMEM((4, 4, SLOT, T), BF),
            pltpu.VMEM((2, N // 2, SLOT, T), BF),
            pltpu.VMEM((N, HEAD // 2 + 1, 2, T), F),
            pltpu.VMEM((N, HEAD // 2 + 1, 2, T), F),
            pltpu.VMEM((SLOT, T), BF),
            pltpu.VMEM((N, SLOT, T), BF),
            pltpu.SemaphoreType.DMA((7,)),
            pltpu.SemaphoreType.DMA((CHUNKS,)),
        ]
        + [pltpu.SemaphoreType.DMA] * 13,
        compiler_params=pltpu.CompilerParams(
            collective_id=0, has_side_effects=True, vmem_limit_bytes=56 << 20
        ),
        name="pair_attention",
    )(
        single.T, key_mask, chain, single_gain, pair_gain, w_bias.T, chain_penalty,
        w_query, w_key, w_value, w_gate, w_out, pair,
    )
    return out.T


def solution(mesh):
    placed = (P("row", "col"), P("row", "col", None), P("row"), P("row")) + (P(),) * 9
    return jax.shard_map(
        per_device, mesh=mesh, in_specs=placed, out_specs=P("row", "col"), check_vma=False
    )
```
